32 devices in a mesh: gx: 8 (over z, x), gy: 4 (over y, core).
Axes of the slice: x: 2, y: 2, z: 4, core: 2. Of those that a mesh axis runs over, the one named last changes fastest.
Arguments:
- adjoint_forcing: float32 [4, 6, 256, 1024], P(None, None, 'gx', 'gy'), may hold values from -6 to 6
- field_mixing: float32 [4, 4], replicated, may hold values from -3 to 3
- time_mixing: float32 [6, 6], replicated, may hold values from -2.5 to 2.5
- kernel_east: float32 [21], replicated, may hold values from 0.1 to 1
- kernel_north: float32 [21], replicated, may hold values from 0.1 to 1
- spatial_modes: bfloat16 [256, 1024, 256], P('gx', 'gy'), may hold values from -0.015625 to 0.015625
- coefficients: float32 [256, 24], P('gy'), may hold values from -6 to 6
Outputs:
- gradient: float32 [256, 24], P('gy')
The draws below stay inside these ranges and needn't reach their ends.
All inputs are finite; a program needn't handle non-finite values.
Results may differ from the reference program's by a relative error of at most 0.0029.
Values sent between devices are 32-bit elements; how exact they have to be, the bound alone decides.
No kernel may reach another device: no remote copies, remote signals or barrier semaphores. Data moves between devices by JAX's collectives and lax.ppermute only.
A program may use at most 64 MiB of HBM per device.

```python
import jax
import jax.numpy as jnp
from jax import lax

FIELDS = 4
LEVELS = 6
MODES = 256
RADIUS = 10
NX = 256
NY = 1024


def spiked(result, stream_key, source, target, blocks, factor):
    owner, partner = [(jnp.arange(result.shape[position]) // (result.shape[position] // blocks)).reshape([-1 if axis == position else 1 for axis in range(result.ndim)]) for position in (source, target)]
    chosen = jax.random.permutation(stream_key, blocks)[partner]
    strong = (owner == chosen) | (owner == (partner + blocks // 2) % blocks)
    return jnp.where(strong, factor * result, result)


def block_levels(stream_key, extent, shards, least, high):
    gain, own = 1.0, jax.random.fold_in(stream_key, 6)
    for axis_at, shards_of in shards:
        draws = jnp.exp(jax.random.uniform(jax.random.fold_in(own, axis_at), (shards_of,), jnp.float32, least / len(shards), high / len(shards)))
        gain = gain * jnp.repeat(draws, extent[axis_at] // shards_of).reshape([-1 if axis == axis_at else 1 for axis in range(len(extent))])
    return gain


def bell_draw(key, extent, spread, limit, pieces=(), dtype=jnp.bfloat16):
    level = block_levels(key, extent, pieces, -0.22, 0.18) if pieces else 1.0
    values = jax.random.normal(key, extent, jnp.float32) * spread * level
    return jnp.minimum(jnp.maximum(values, -limit), limit).astype(dtype)


def bell_draw_with(key, dims, width, limit, shards, heavy, held_as=jnp.bfloat16):
    values = width * jax.random.normal(key, dims, jnp.float32)
    if shards:
        values = values * block_levels(key, dims, shards, -0.22, 0.18)
    return jnp.clip(spiked(values, jax.random.fold_in(key, 3), *heavy), -limit, limit).astype(held_as)


def setup_inputs(seed: int = 0) -> dict:
    streams_of = jax.random.split(jax.random.key(seed), 8)
    adjoint_forcing = bell_draw(streams_of[0], (FIELDS, LEVELS, NX, NY), 1.0, 6.0, ((2, 8), (3, 4)), jnp.float32)
    field_mixing = bell_draw(streams_of[1], (FIELDS, FIELDS), FIELDS ** -0.5, 3.0, (), jnp.float32)
    time_mixing = bell_draw(streams_of[2], (LEVELS, LEVELS), LEVELS ** -0.5, 2.5, (), jnp.float32)
    kernel_east = jnp.clip(jax.random.uniform(streams_of[3], (2 * RADIUS + 1,), jnp.float32, 0.1, 1.0), 0.1, 1.0)
    kernel_north = jnp.clip(jax.random.uniform(streams_of[4], (2 * RADIUS + 1,), jnp.float32, 0.1, 1.0), 0.1, 1.0)
    spatial_modes = bell_draw_with(streams_of[5], (NX, NY, MODES), (NX * NY) ** -0.5, 0.015625, ((0, 8), (1, 4)), (1, 2, 4, 2.0))
    coefficients = bell_draw(streams_of[6], (MODES, FIELDS * LEVELS), 1.0, 6.0, ((0, 4),), jnp.float32)
    return {"adjoint_forcing": adjoint_forcing, "field_mixing": field_mixing, "time_mixing": time_mixing, "kernel_east": kernel_east, "kernel_north": kernel_north, "spatial_modes": spatial_modes, "coefficients": coefficients}


def smooth(field, taps, axis, reach):
    count = field.shape[axis]
    pads = [(0, 0)] * field.ndim
    pads[axis] = (reach, reach)
    padded = jnp.pad(field, pads)
    total = jnp.zeros(field.shape, jnp.float32)
    for j in range(2 * reach + 1):
        total = total + taps[j] * lax.slice_in_dim(padded, j, j + count, axis=axis)
    return total


def reference(adjoint_forcing, field_mixing, time_mixing, kernel_east, kernel_north, spatial_modes, coefficients):
    mixed = jnp.einsum("gf,st,gsxy->ftxy", field_mixing, time_mixing, adjoint_forcing, precision=lax.Precision.HIGHEST)
    along_x = smooth(mixed, kernel_east, 2, RADIUS)
    smoothed = smooth(along_x, kernel_north, 3, RADIUS).astype(jnp.bfloat16)
    flat_state = smoothed.reshape(FIELDS * LEVELS, NX * NY)
    flat_modes = spatial_modes.reshape(NX * NY, MODES)
    projection = lax.dot_general(flat_modes, flat_state, (((0,), (1,)), ((), ())), preferred_element_type=jnp.float32)
    return coefficients + projection
```

```python
import functools

import jax
import jax.numpy as jnp
from jax import lax
from jax.experimental import pallas as pl
from jax.experimental.pallas import tpu as pltpu
from jax.sharding import PartitionSpec as P

F32, BF16 = jnp.float32, jnp.bfloat16
NT = (((1,), (1,)), ((), ()))
TN = (((0,), (0,)), ((), ()))
NN = (((1,), (0,)), ((), ()))
STRIP = 16


def dot(a, b, dims=NN):
    return lax.dot_general(a, b, dims, preferred_element_type=F32)


def halves(v):
    high = v.astype(BF16)
    return high, (v - high.astype(F32)).astype(BF16)


def dot2(a, b, dims=NN):
    (ah, al), (bh, bl) = a, b
    return dot(ah, bh, dims) + dot(ah, bl, dims) + dot(al, bh, dims)


def iota(shape, dim):
    return lax.broadcasted_iota(jnp.int32, shape, dim)


def turn_kernel(reach, a_ref, t_ref, s1_ref, s2_ref):
    t_ref[...] = jnp.swapaxes(a_ref[...], 0, 1)
    odd = lax.axis_index("gx") % 2
    last = t_ref.shape[0] - 1
    for n in range(reach):
        s1_ref[n] = t_ref[odd * n + (1 - odd) * (last - n)]
        s2_ref[n] = t_ref[(1 - odd) * n + odd * (last - n)]


def strip_kernel(reach, t_ref, core_ref, chip_ref):
    width_x, channels, width_y = t_ref.shape
    odd = lax.axis_index("gy") % 2
    row, col = iota((2 * STRIP, width_y), 0), iota((2 * STRIP, width_y), 1)
    to_core = row < STRIP
    at = jnp.where(to_core, row, row - STRIP)
    low = jnp.where(to_core, odd, 1 - odd) == 1
    wanted = at + jnp.where(low, 0, width_y - reach)
    pick = jnp.where((col == wanted) & (at < reach), 1.0, 0.0).astype(BF16)
    data = t_ref[...].reshape(width_x * channels, width_y)
    high, rest = halves(data)
    low_part = (data - high.astype(F32) - rest.astype(F32)).astype(BF16)
    strips = dot(pick, high, NT) + dot(pick, rest, NT) + dot(pick, low_part, NT)
    core_ref[...] = strips[:STRIP]
    chip_ref[...] = strips[STRIP:]


def band_kernel(reach, north_ref, field_ref, time_ref, t_ref, y_ref, bh_ref, bl_ref, eh_ref, el_ref, mix_ref):
    width_x, channels, width_y = t_ref.shape
    odd = lax.axis_index("gy") % 2
    shift = iota((width_y, width_y), 0) - iota((width_y, width_y), 1) + reach
    row = iota((2 * STRIP, width_y), 0)
    from_core = row < STRIP
    at = jnp.where(from_core, row, row - STRIP)
    left = jnp.where(from_core, odd, 1 - odd) == 1
    source = jnp.where(left, at - reach, width_y + at)
    edge_shift = jnp.where(at < reach, source - iota((2 * STRIP, width_y), 1) + reach, -1)
    band = jnp.zeros((width_y, width_y), F32)
    edge = jnp.zeros((2 * STRIP, width_y), F32)
    for j in range(2 * reach + 1):
        band = jnp.where(shift == j, north_ref[j], band)
        edge = jnp.where(edge_shift == j, north_ref[j], edge)
    band, edge = halves(band), halves(edge)
    bh_ref[...], bl_ref[...] = band
    eh_ref[...], el_ref[...] = edge
    y_ref[...] = dot2(halves(t_ref[...].reshape(width_x * channels, width_y)), band).reshape(t_ref.shape)
    fields, levels = field_ref.shape[0], time_ref.shape[0]
    out, into = iota((channels, channels), 0), iota((channels, channels), 1)
    by_field = jnp.zeros((channels, channels), F32)
    by_time = jnp.zeros((channels, channels), F32)
    for g in range(fields):
        for f in range(fields):
            here = (into // levels == g) & (out // levels == f)
            by_field = jnp.where(here, field_ref[g, f], by_field)
    for s in range(levels):
        for t in range(levels):
            by_time = jnp.where((into % levels == s) & (out % levels == t), time_ref[s, t], by_time)
    mix_ref[...] = by_field * by_time


def corner_kernel(reach, channels, core_ref, chip_ref, strips_ref, c1_ref, c2_ref):
    odd = lax.axis_index("gx") % 2
    strips = jnp.concatenate([core_ref[...], chip_ref[...]], axis=0)
    strips_ref[...] = strips
    top = strips[:, : reach * channels]
    bottom = strips[:, strips.shape[1] - reach * channels :]
    c1_ref[...] = jnp.where(odd == 1, top, bottom)
    c2_ref[...] = jnp.where(odd == 1, bottom, top)


def split_rows(v):
    high = v.astype(BF16).astype(F32)
    return jnp.concatenate([high, v - high], axis=0).astype(BF16)


def tile_kernel(reach, east_ref, y_ref, strips_ref, eh_ref, el_ref, modes_ref, p_ref, total, smooth):
    width_x, channels, width_y = y_ref.shape
    more = dot2(halves(strips_ref[...]), (eh_ref[...], el_ref[...]), TN)
    total[...] = y_ref[...] + more.reshape(y_ref.shape)
    acc = jnp.zeros((2 * channels, modes_ref.shape[2]), F32)
    for x in range(width_x):
        value = None
        for j in range(2 * reach + 1):
            if 0 <= x + j - reach < width_x:
                term = east_ref[j] * total[x + j - reach]
                value = term if value is None else value + term
        smooth[x] = split_rows(value)
    for x in range(width_x):
        acc = acc + dot(smooth[x], modes_ref[x])
    p_ref[...] = acc[:channels] + acc[channels:]


def halo_kernel(reach, owned, east_ref, p_ref, r1_ref, r2_ref, c1_ref, c2_ref, bh_ref, bl_ref, eh_ref, el_ref, modes_ref, out_ref, by_y, by_corner, smooth):
    channels, width_y = r1_ref.shape[1:]
    width_x, _, modes = modes_ref.shape
    odd = lax.axis_index("gx") % 2
    band, edge = (bh_ref[...], bl_ref[...]), (eh_ref[...], el_ref[...])
    acc = jnp.zeros((2 * channels, modes), F32)
    for r_ref, c_ref, left in ((r1_ref, c1_ref, odd), (r2_ref, c2_ref, 1 - odd)):
        rows = r_ref[...].reshape(reach * channels, width_y)
        by_y[...] = dot2(halves(rows), band).reshape(r_ref.shape)
        by_corner[...] = dot2(halves(c_ref[...]), edge, TN).reshape(r_ref.shape)
        taps = [jnp.where(left == 1, east_ref[d], east_ref[2 * reach - d]) for d in range(reach)]
        came = [by_y[n] + by_corner[left * (reach - 1 - n) + (1 - left) * n] for n in range(reach)]
        for m in range(reach):
            value = taps[m] * came[0]
            for n in range(1, m + 1):
                value = value + taps[m - n] * came[n]
            smooth[m] = split_rows(value)
        for m in range(reach):
            acc = acc + dot(smooth[m], modes_ref[left * (reach - 1 - m) + (1 - left) * (width_x - reach + m)])
    total = p_ref[...] + acc[:channels] + acc[channels:]
    folds = 128 // owned
    rows = channels // folds
    for g in range(modes // owned):
        piece = jnp.concatenate(
            [total[k * rows : (k + 1) * rows, g * owned : (g + 1) * owned] for k in range(folds)], axis=1
        )
        for k in range(out_ref.shape[0]):
            out_ref[k, g] = piece


def sum_kernel(parts_ref, mix_ref, coefficients_ref, out_ref):
    channels, owned = out_ref.shape
    folds = 128 // owned
    rows = channels // folds
    total = jnp.sum(parts_ref[...], axis=0)
    value = coefficients_ref[...]
    for k in range(folds):
        mixed = lax.dot_general(
            mix_ref[:, k * rows : (k + 1) * rows], total, NN, precision=lax.Precision.HIGHEST, preferred_element_type=F32
        )
        value = value + mixed[:, k * owned : (k + 1) * owned]
    out_ref[...] = value


def call(body, ins, outs, scratch=(), flops=0):
    args, specs = [], []
    for item in ins:
        scalar = isinstance(item, tuple)
        if scalar:
            args.append(item[0])
            specs.append(pl.BlockSpec(memory_space=pltpu.SMEM))
        else:
            args.append(pltpu.with_memory_space_constraint(item, pltpu.VMEM))
            specs.append(pl.BlockSpec(memory_space=pltpu.VMEM))
    return pl.pallas_call(
        body,
        out_shape=[pltpu.VMEM(shape, dtype) for shape, dtype in outs],
        in_specs=specs,
        out_specs=[pl.BlockSpec(memory_space=pltpu.VMEM)] * len(outs),
        scratch_shapes=list(scratch),
        compiler_params=pltpu.CompilerParams(vmem_limit_bytes=24 << 20),
        cost_estimate=pl.CostEstimate(flops=flops, bytes_accessed=1 << 20, transcendentals=0),
    )(*args)


def pairs(count, first):
    found = []
    for low in range(first, count - 1, 2):
        found += [(low, low + 1), (low + 1, low)]
    return found


def local(adjoint_forcing, field_mixing, time_mixing, kernel_east, kernel_north, spatial_modes, coefficients):
    fields, levels, width_x, width_y = adjoint_forcing.shape
    channels, modes, owned = fields * levels, spatial_modes.shape[2], coefficients.shape[0]
    reach = (kernel_east.shape[0] - 1) // 2
    count_x, count_y = lax.axis_size("gx"), lax.axis_size("gy")
    raw = adjoint_forcing.reshape(channels, width_x, width_y)
    slab = (reach, channels, width_y)
    t, s1, s2 = call(
        functools.partial(turn_kernel, reach), [raw], [((width_x, channels, width_y), F32), (slab, F32), (slab, F32)]
    )
    r1 = lax.ppermute(s1, "gx", pairs(count_x, 0))
    strip = ((STRIP, width_x * channels), F32)
    core, chip = call(functools.partial(strip_kernel, reach), [t], [strip, strip])
    core = lax.ppermute(core, "gy", pairs(count_y, 0))
    chip = lax.ppermute(chip, "gy", pairs(count_y, 1))
    r2 = lax.ppermute(s2, "gx", pairs(count_x, 1))
    y, bh, bl, eh, el, mix = call(
        functools.partial(band_kernel, reach),
        [(kernel_north, True), (field_mixing, True), (time_mixing, True), t],
        [
            (t.shape, F32),
            ((width_y, width_y), BF16),
            ((width_y, width_y), BF16),
            ((2 * STRIP, width_y), BF16),
            ((2 * STRIP, width_y), BF16),
            ((channels, channels), F32),
        ],
    )
    corner = ((2 * STRIP, reach * channels), F32)
    strips, c1, c2 = call(
        functools.partial(corner_kernel, reach, channels),
        [core, chip],
        [((2 * STRIP, width_x * channels), F32), corner, corner],
    )
    c1 = lax.ppermute(c1, "gx", pairs(count_x, 0))
    c2 = lax.ppermute(c2, "gx", pairs(count_x, 1))
    (share,) = call(
        functools.partial(tile_kernel, reach),
        [(kernel_east, True), y, strips, eh, el, spatial_modes],
        [((channels, modes), F32)],
        [pltpu.VMEM(t.shape, F32), pltpu.VMEM((width_x, 2 * channels, width_y), BF16)],
    )
    folds = 128 // owned
    (out,) = call(
        functools.partial(halo_kernel, reach, owned),
        [(kernel_east, True), share, r1, r2, c1, c2, bh, bl, eh, el, spatial_modes],
        [((count_x, count_y, channels // folds, 128), F32)],
        [pltpu.VMEM(slab, F32), pltpu.VMEM(slab, F32), pltpu.VMEM((reach, 2 * channels, width_y), BF16)],
    )
    out = out.reshape((count_x * count_y,) + out.shape[2:])
    parts = lax.all_to_all(out, ("gx", "gy"), 0, 0, tiled=True)
    (gradient,) = call(sum_kernel, [parts, mix, coefficients.T], [((channels, owned), F32)])
    return gradient.T


def solution(mesh):
    in_specs = (P(None, None, "gx", "gy"), P(), P(), P(), P(), P("gx", "gy", None), P("gy", None))
    out_specs = P("gy", None)
    return jax.shard_map(local, mesh=mesh, in_specs=in_specs, out_specs=out_specs, check_vma=False)
```

```python
import functools

import jax
import jax.numpy as jnp
from jax import lax
from jax.experimental import pallas as pl
from jax.experimental.pallas import tpu as pltpu
from jax.sharding import PartitionSpec as P

F32, BF16 = jnp.float32, jnp.bfloat16
NN = (((1,), (0,)), ((), ()))
NT = (((1,), (1,)), ((), ()))
TN = (((0,), (0,)), ((), ()))
STRIP = 12
EDGE = 32


def dot(a, b, dims=NN):
    return lax.dot_general(a, b, dims, preferred_element_type=F32)


def halves(v):
    high = v.astype(BF16)
    return high, (v - high.astype(F32)).astype(BF16)


def dot2(a, b, dims=NN):
    (ah, al), (bh, bl) = a, b
    return dot(ah, bh, dims) + dot(ah, bl, dims) + dot(al, bh, dims)


def iota(shape, dim):
    return lax.broadcasted_iota(jnp.int32, shape, dim)


def stacked(v):
    high = v.astype(BF16).astype(F32)
    parts = [high, v - high, high]
    if (3 * v.shape[0]) % 16:
        parts.append(jnp.zeros((-3 * v.shape[0] % 96, v.shape[1]), F32))
    return jnp.concatenate(parts, axis=0).astype(BF16)


def wide(m):
    high = m.astype(BF16).astype(F32)
    parts = [high, high, m - high]
    if (3 * m.shape[1]) % 16:
        parts.append(jnp.zeros((m.shape[0], -3 * m.shape[1] % 96), F32))
    return jnp.concatenate(parts, axis=1).astype(BF16)


def turn_kernel(reach, a_ref, t_ref, s1_ref):
    t_ref[...] = jnp.swapaxes(a_ref[...], 0, 1)
    odd = lax.axis_index("gx") % 2
    s1_ref[...] = t_ref[pl.ds((1 - odd) * (t_ref.shape[0] - reach), reach)]


def strip_kernel(reach, t_ref, core_ref, chip_ref):
    width_x, channels, width_y = t_ref.shape
    odd = lax.axis_index("gy") % 2
    row, col = iota((EDGE, width_y), 0), iota((EDGE, width_y), 1)
    to_core = row < STRIP
    at = jnp.where(to_core, row, row - STRIP)
    low = jnp.where(to_core, odd, 1 - odd) == 1
    wanted = at + jnp.where(low, 0, width_y - reach)
    pick = jnp.where((col == wanted) & (at < reach), 1.0, 0.0).astype(BF16)
    data = t_ref[...].reshape(width_x * channels, width_y)
    high, rest = halves(data)
    low_part = (data - high.astype(F32) - rest.astype(F32)).astype(BF16)
    strips = dot(pick, high, NT) + dot(pick, rest, NT) + dot(pick, low_part, NT)
    core_ref[...] = strips[:STRIP]
    chip_ref[...] = strips[STRIP : 2 * STRIP]


def band_kernel(
    reach, east_hbm, north_hbm, field_hbm, time_hbm, a_ref, y_ref, bh_ref, bl_ref, eh_ref, el_ref, x_ref, mix_ref, taps_ref,
    east_ref, north_ref, field_ref, time_ref, sem,
):
    copies = [
        pltpu.make_async_copy(source, target, sem.at[i])
        for i, (source, target) in enumerate(
            ((east_hbm, east_ref), (north_hbm, north_ref), (field_hbm, field_ref), (time_hbm, time_ref))
        )
    ]
    for copy in copies:
        copy.start()
    channels, width_x, width_y = a_ref.shape
    span = 2 * reach + 1
    odd = lax.axis_index("gy") % 2
    shift = iota((width_y, width_y), 0) - iota((width_y, width_y), 1) + reach
    row = iota((EDGE, width_y), 0)
    from_core = row < STRIP
    at = jnp.where(from_core, row, row - STRIP)
    left = jnp.where(from_core, odd, 1 - odd) == 1
    source = jnp.where(left, at - reach, width_y + at)
    edge_shift = jnp.where(at < reach, source - iota((EDGE, width_y), 1) + reach, -1)
    x_shift = iota((width_x, width_x), 1) - iota((width_x, width_x), 0) + reach
    data = halves(a_ref[...].reshape(channels * width_x, width_y))
    for copy in copies:
        copy.wait()
    first = iota((8, width_y), 1)
    base = jnp.zeros((8, width_y), F32)
    edge = jnp.zeros((EDGE, width_y), F32)
    along = jnp.zeros((width_x, width_x), F32)
    for j in range(span):
        tap = north_ref[j]
        base = jnp.where(first == (reach - j) % width_y, tap, base)
        edge = jnp.where(edge_shift == j, tap, edge)
        along = jnp.where(x_shift == j, east_ref[j], along)
        taps_ref[j] = jnp.full(taps_ref.shape[1:], east_ref[j], F32)
    rolled = pltpu.roll(jnp.broadcast_to(base[:1], (width_y, width_y)), 0, 1, stride=1, stride_axis=0)
    band = halves(jnp.where((shift >= 0) & (shift < span), rolled, 0.0))
    edge = halves(edge)
    bh_ref[...], bl_ref[...] = band
    eh_ref[...], el_ref[...] = edge
    x_ref[...] = wide(along)
    fields, levels = field_ref.shape[0], time_ref.shape[0]
    rows = mix_ref.shape[0]
    out, into = iota((rows, channels), 0), iota((rows, channels), 1)
    by_field = jnp.zeros((rows, channels), F32)
    by_time = jnp.zeros((rows, channels), F32)
    for g in range(fields):
        for f in range(fields):
            by_field = jnp.where((into // levels == g) & (out // levels == f), field_ref[g, f], by_field)
    for s in range(levels):
        for t in range(levels):
            by_time = jnp.where((into % levels == s) & (out % levels == t), time_ref[s, t], by_time)
    mix_ref[...] = wide(by_field * by_time)
    y_ref[...] = dot2(data, band).reshape(a_ref.shape)


def joined(core, chip):
    return jnp.concatenate([core, chip, jnp.zeros((EDGE - 2 * STRIP, core.shape[1]), F32)], axis=0)


def corner_kernel(reach, t_ref, core_ref, chip_ref, s2_ref):
    width_x, channels, width_y = t_ref.shape
    odd = lax.axis_index("gx") % 2
    s2_ref[:reach] = t_ref[pl.ds(odd * (width_x - reach), reach)]
    strips = joined(core_ref[...], chip_ref[...])[: 2 * STRIP]
    top = strips[:, : reach * channels]
    bottom = strips[:, (width_x - reach) * channels :]
    rows = jnp.where(odd == 1, bottom, top)
    s2_ref[reach] = jnp.concatenate([rows, jnp.zeros((2 * STRIP, width_y - reach * channels), F32)], axis=1)


def tile_kernel(reach, modes_hbm, y_ref, core_ref, chip_ref, eh_ref, el_ref, x_ref, mix_ref, s_ref, p_ref, modes_ref, sem):
    channels, width_x, width_y = y_ref.shape
    blocks = sem.shape[0]
    size = width_x // blocks
    copies = [
        pltpu.make_async_copy(modes_hbm.at[pl.ds(b * size, size)], modes_ref.at[pl.ds(b * size, size)], sem.at[b])
        for b in range(blocks)
    ]
    for copy in copies:
        copy.start()
    more = dot2(halves(joined(core_ref[...], chip_ref[...])), (eh_ref[...], el_ref[...]), TN)
    y = y_ref[...] + jnp.swapaxes(more.reshape(width_x, channels, width_y), 0, 1)
    along = x_ref[...]
    smooth = jnp.stack([dot(along, stacked(y[c])) for c in range(channels)])
    s_ref[...] = jnp.swapaxes(smooth, 0, 1)
    mix = mix_ref[...]
    acc = jnp.zeros((mix.shape[0], modes_ref.shape[2]), F32)
    inner = [dot(mix, stacked(s_ref[x])).astype(BF16) for x in range(reach, width_x - reach)]
    for copy in copies:
        copy.wait()
    for x in range(reach, width_x - reach):
        acc = acc + dot(inner[x - reach], modes_ref[x])
    p_ref[...] = acc


def side(reach, left, rows, corners, s_ref, taps_ref, bh_ref, bl_ref, eh_ref, el_ref, mix_ref, modes_ref, by_y):
    width_x, channels, width_y = s_ref.shape
    by = dot2(halves(rows.reshape(reach * channels, width_y)), (bh_ref[...], bl_ref[...]))
    by = by + dot2(halves(corners), (eh_ref[...], el_ref[...]), TN)
    by_y[...] = by.reshape(reach, channels, width_y)
    split = (channels // 8, 8, width_y)
    came = [by_y[left * (reach - 1 - n) + (1 - left) * n].reshape(split) for n in range(reach)]
    taps = [taps_ref[left * d + (1 - left) * (2 * reach - d)][None] for d in range(reach)]
    mix = mix_ref[...]
    acc = jnp.zeros((mix.shape[0], modes_ref.shape[2]), F32)
    for m in range(reach):
        x = left * (reach - 1 - m) + (1 - left) * (width_x - reach + m)
        value = s_ref[x].reshape(split)
        for n in range(m + 1):
            value = value + taps[m - n] * came[n]
        mixed = dot(mix, stacked(value.reshape(channels, width_y))).astype(BF16)
        acc = acc + dot(mixed, modes_ref[x])
    return acc


def first_kernel(reach, p_ref, r_ref, core_ref, chip_ref, s_ref, *rest):
    *refs, out_ref, by_y = rest
    odd = lax.axis_index("gx") % 2
    corners = joined(core_ref[...], chip_ref[...])
    out_ref[...] = p_ref[...] + side(reach, odd, r_ref[...], corners, s_ref, *refs, by_y)


def second_kernel(reach, owned, p_ref, r_ref, s_ref, *rest):
    *refs, out_ref, by_y = rest
    odd = lax.axis_index("gx") % 2
    _, channels, width_y = s_ref.shape
    corners = jnp.concatenate([r_ref[reach], jnp.zeros((EDGE - 2 * STRIP, width_y), F32)], axis=0)[:, : reach * channels]
    total = p_ref[...] + side(reach, 1 - odd, r_ref[:reach], corners, s_ref, *refs, by_y)
    folds = 128 // owned
    rows = channels // folds
    for g in range(total.shape[1] // owned):
        piece = jnp.concatenate(
            [total[k * rows : (k + 1) * rows, g * owned : (g + 1) * owned] for k in range(folds)], axis=1
        )
        for k in range(out_ref.shape[0]):
            out_ref[k, g] = piece


def sum_kernel(parts_ref, coefficients_ref, out_ref):
    channels, owned = out_ref.shape
    folds = 128 // owned
    total = jnp.sum(parts_ref[...], axis=0)
    pieces = [total[:, k * owned : (k + 1) * owned] for k in range(folds)]
    out_ref[...] = coefficients_ref[...] + jnp.concatenate(pieces, axis=0)


def vmem(array):
    return pltpu.with_memory_space_constraint(array, pltpu.VMEM)


def call(body, ins, outs, scratch=(), flops=0, outside=0, keep=True):
    args = [item if i < outside else vmem(item) for i, item in enumerate(ins)]
    specs = [pl.BlockSpec(memory_space=pl.ANY if i < outside else pltpu.VMEM) for i in range(len(ins))]
    make = pltpu.VMEM if keep else jax.ShapeDtypeStruct
    return pl.pallas_call(
        body,
        out_shape=[make(shape, dtype) for shape, dtype in outs],
        in_specs=specs,
        out_specs=[pl.BlockSpec(memory_space=pltpu.VMEM)] * len(outs),
        scratch_shapes=list(scratch),
        compiler_params=pltpu.CompilerParams(vmem_limit_bytes=24 << 20),
        cost_estimate=pl.CostEstimate(flops=flops, bytes_accessed=1 << 20, transcendentals=0),
    )(*args)


def pairs(count, first):
    found = []
    for low in range(first, count - 1, 2):
        found += [(low, low + 1), (low + 1, low)]
    return found


def local(adjoint_forcing, field_mixing, time_mixing, kernel_east, kernel_north, spatial_modes, coefficients):
    fields, levels, width_x, width_y = adjoint_forcing.shape
    channels, modes, owned = fields * levels, spatial_modes.shape[2], coefficients.shape[0]
    reach = (kernel_east.shape[0] - 1) // 2
    count_x, count_y = lax.axis_size("gx"), lax.axis_size("gy")
    raw = vmem(adjoint_forcing.reshape(channels, width_x, width_y))
    slab = (reach, channels, width_y)
    full = ((width_x, channels, width_y), F32)
    t, s1 = call(functools.partial(turn_kernel, reach), [raw], [full, (slab, F32)])
    r1 = lax.ppermute(s1, "gx", pairs(count_x, 0))
    strip = ((STRIP, width_x * channels), F32)
    core, chip = call(functools.partial(strip_kernel, reach), [t], [strip, strip])
    core = lax.ppermute(core, "gy", pairs(count_y, 0))
    chip = lax.ppermute(chip, "gy", pairs(count_y, 1))
    edge = ((EDGE, width_y), BF16)
    band = ((width_y, width_y), BF16)
    wide_rows = -(-channels // 16) * 16
    y, bh, bl, eh, el, along, mix, taps = call(
        functools.partial(band_kernel, reach),
        [kernel_east, kernel_north, field_mixing, time_mixing, raw],
        [
            ((channels, width_x, width_y), F32),
            band,
            band,
            edge,
            edge,
            ((width_x, 3 * width_x + -3 * width_x % 96), BF16),
            ((wide_rows, 3 * channels + -3 * channels % 96), BF16),
            ((2 * reach + 1, 8, width_y), F32),
        ],
        [
            pltpu.SMEM(kernel_east.shape, F32),
            pltpu.SMEM(kernel_north.shape, F32),
            pltpu.SMEM(field_mixing.shape, F32),
            pltpu.SMEM(time_mixing.shape, F32),
            pltpu.SemaphoreType.DMA((4,)),
        ],
        outside=4,
    )
    (s2,) = call(functools.partial(corner_kernel, reach), [t, core, chip], [((reach + 1, channels, width_y), F32)])
    r2 = lax.ppermute(s2, "gx", pairs(count_x, 1))
    strip = ((STRIP, reach * channels), F32)
    core1, chip1 = call(functools.partial(strip_kernel, reach), [r1], [strip, strip])
    core1 = lax.ppermute(core1, "gy", pairs(count_y, 0))
    chip1 = lax.ppermute(chip1, "gy", pairs(count_y, 1))
    share = ((wide_rows, modes), F32)
    smooth, inner, held = call(
        functools.partial(tile_kernel, reach),
        [spatial_modes, y, core, chip, eh, el, along, mix],
        [full, share, (spatial_modes.shape, BF16)],
        [pltpu.SemaphoreType.DMA((4,))],
        outside=1,
    )
    both = [smooth, taps, bh, bl, eh, el, mix, held]
    (partial,) = call(
        functools.partial(first_kernel, reach), [inner, r1, core1, chip1, *both], [share], [pltpu.VMEM(slab, F32)]
    )
    folds = 128 // owned
    (out,) = call(
        functools.partial(second_kernel, reach, owned),
        [partial, r2, *both],
        [((count_x, count_y, channels // folds, 128), F32)],
        [pltpu.VMEM(slab, F32)],
    )
    out = out.reshape((count_x * count_y,) + out.shape[2:])
    parts = lax.all_to_all(out, ("gx", "gy"), 0, 0, tiled=True)
    (gradient,) = call(sum_kernel, [parts, coefficients.T], [((channels, owned), F32)], keep=False)
    return gradient.T


def solution(mesh):
    in_specs = (P(None, None, "gx", "gy"), P(), P(), P(), P(), P("gx", "gy", None), P("gy", None))
    out_specs = P("gy", None)
    return jax.shard_map(local, mesh=mesh, in_specs=in_specs, out_specs=out_specs, check_vma=False)
```

```python
import functools

import jax
import jax.numpy as jnp
from jax import lax
from jax.experimental import pallas as pl
from jax.experimental.pallas import tpu as pltpu
from jax.sharding import PartitionSpec as P

F32, BF16 = jnp.float32, jnp.bfloat16
NN = (((1,), (0,)), ((), ()))
NT = (((1,), (1,)), ((), ()))
TN = (((0,), (0,)), ((), ()))
STRIP = 12
EDGE = 32


def dot(a, b, dims=NN):
    return lax.dot_general(a, b, dims, preferred_element_type=F32)


def halves(v):
    high = v.astype(BF16)
    return high, (v - high.astype(F32)).astype(BF16)


def dot2(a, b, dims=NN):
    (ah, al), (bh, bl) = a, b
    return dot(ah, bh, dims) + dot(ah, bl, dims) + dot(al, bh, dims)


def iota(shape, dim):
    return lax.broadcasted_iota(jnp.int32, shape, dim)


def stacked(v):
    high = v.astype(BF16).astype(F32)
    parts = [high, v - high, high]
    if (3 * v.shape[0]) % 16:
        parts.append(jnp.zeros((-3 * v.shape[0] % 96, v.shape[1]), F32))
    return jnp.concatenate(parts, axis=0).astype(BF16)


def wide(m):
    high = m.astype(BF16).astype(F32)
    parts = [high, high, m - high]
    if (3 * m.shape[1]) % 16:
        parts.append(jnp.zeros((m.shape[0], -3 * m.shape[1] % 96), F32))
    return jnp.concatenate(parts, axis=1).astype(BF16)


def turn_kernel(reach, a_ref, t_ref, s1_ref):
    t_ref[...] = jnp.swapaxes(a_ref[...], 0, 1)
    odd = lax.axis_index("gx") % 2
    s1_ref[...] = t_ref[pl.ds((1 - odd) * (t_ref.shape[0] - reach), reach)]


def strip_kernel(reach, t_ref, core_ref, chip_ref):
    width_x, channels, width_y = t_ref.shape
    odd = lax.axis_index("gy") % 2
    row, col = iota((EDGE, width_y), 0), iota((EDGE, width_y), 1)
    to_core = row < STRIP
    at = jnp.where(to_core, row, row - STRIP)
    low = jnp.where(to_core, odd, 1 - odd) == 1
    wanted = at + jnp.where(low, 0, width_y - reach)
    pick = jnp.where((col == wanted) & (at < reach), 1.0, 0.0).astype(BF16)
    data = t_ref[...].reshape(width_x * channels, width_y)
    high, rest = halves(data)
    low_part = (data - high.astype(F32) - rest.astype(F32)).astype(BF16)
    strips = dot(pick, high, NT) + dot(pick, rest, NT) + dot(pick, low_part, NT)
    core_ref[...] = strips[:STRIP]
    chip_ref[...] = strips[STRIP : 2 * STRIP]


def band_kernel(
    reach, east_hbm, north_hbm, field_hbm, time_hbm, modes_hbm, t_ref, y_ref, bh_ref, bl_ref, eh_ref, el_ref, x_ref, mix_ref, taps_ref,
    modes_ref, east_ref, north_ref, field_ref, time_ref, sem,
):
    copies = [
        pltpu.make_async_copy(source, target, sem.at[i])
        for i, (source, target) in enumerate(
            ((east_hbm, east_ref), (north_hbm, north_ref), (field_hbm, field_ref), (time_hbm, time_ref))
        )
    ]
    for copy in copies:
        copy.start()
    width_x, channels, width_y = t_ref.shape
    half = width_x // 2
    loads = [
        pltpu.make_async_copy(modes_hbm.at[pl.ds(i * half, half)], modes_ref.at[pl.ds(i * half, half)], sem.at[len(copies) + i])
        for i in range(2)
    ]
    for load in loads:
        load.start()
    span = 2 * reach + 1
    odd = lax.axis_index("gy") % 2
    shift = iota((width_y, width_y), 0) - iota((width_y, width_y), 1) + reach
    row = iota((EDGE, width_y), 0)
    from_core = row < STRIP
    at = jnp.where(from_core, row, row - STRIP)
    left = jnp.where(from_core, odd, 1 - odd) == 1
    source = jnp.where(left, at - reach, width_y + at)
    edge_shift = jnp.where(at < reach, source - iota((EDGE, width_y), 1) + reach, -1)
    x_shift = iota((width_x, width_x), 1) - iota((width_x, width_x), 0) + reach
    data = halves(t_ref[...].reshape(width_x * channels, width_y))
    for copy in copies:
        copy.wait()
    first = iota((8, width_y), 1)
    base = jnp.zeros((8, width_y), F32)
    edge = jnp.zeros((EDGE, width_y), F32)
    along = jnp.zeros((width_x, width_x), F32)
    for j in range(span):
        tap = north_ref[j]
        base = jnp.where(first == (reach - j) % width_y, tap, base)
        edge = jnp.where(edge_shift == j, tap, edge)
        along = jnp.where(x_shift == j, east_ref[j], along)
        taps_ref[j] = jnp.full(taps_ref.shape[1:], east_ref[j], F32)
    rolled = pltpu.roll(jnp.broadcast_to(base[:1], (width_y, width_y)), 0, 1, stride=1, stride_axis=0)
    band = halves(jnp.where((shift >= 0) & (shift < span), rolled, 0.0))
    edge = halves(edge)
    bh_ref[...], bl_ref[...] = band
    eh_ref[...], el_ref[...] = edge
    x_ref[...] = wide(along)
    fields, levels = field_ref.shape[0], time_ref.shape[0]
    rows = mix_ref.shape[0]
    out, into = iota((rows, channels), 0), iota((rows, channels), 1)
    by_field = jnp.zeros((rows, channels), F32)
    by_time = jnp.zeros((rows, channels), F32)
    for g in range(fields):
        for f in range(fields):
            by_field = jnp.where((into // levels == g) & (out // levels == f), field_ref[g, f], by_field)
    for s in range(levels):
        for t in range(levels):
            by_time = jnp.where((into % levels == s) & (out % levels == t), time_ref[s, t], by_time)
    mix_ref[...] = wide(by_field * by_time)
    y_ref[...] = jnp.swapaxes(dot2(data, band).reshape(t_ref.shape), 0, 1)
    for load in loads:
        load.wait()


def joined(core, chip):
    return jnp.concatenate([core, chip, jnp.zeros((EDGE - 2 * STRIP, core.shape[1]), F32)], axis=0)


def corner_kernel(reach, t_ref, core_ref, chip_ref, s2_ref):
    width_x, channels, width_y = t_ref.shape
    odd = lax.axis_index("gx") % 2
    s2_ref[:reach] = t_ref[pl.ds(odd * (width_x - reach), reach)]
    strips = joined(core_ref[...], chip_ref[...])[: 2 * STRIP]
    top = strips[:, : reach * channels]
    bottom = strips[:, (width_x - reach) * channels :]
    rows = jnp.where(odd == 1, bottom, top)
    s2_ref[reach] = jnp.concatenate([rows, jnp.zeros((2 * STRIP, width_y - reach * channels), F32)], axis=1)


def tile_kernel(reach, y_ref, core_ref, chip_ref, eh_ref, el_ref, x_ref, mix_ref, modes_ref, s_ref, p_ref):
    channels, width_x, width_y = y_ref.shape
    more = dot2(halves(joined(core_ref[...], chip_ref[...])), (eh_ref[...], el_ref[...]), TN)
    y = y_ref[...] + jnp.swapaxes(more.reshape(width_x, channels, width_y), 0, 1)
    along = x_ref[...]
    smooth = jnp.stack([dot(along, stacked(y[c])) for c in range(channels)])
    s_ref[...] = jnp.swapaxes(smooth, 0, 1)
    mix = mix_ref[...]
    inner = [dot(mix, stacked(s_ref[x])).astype(BF16) for x in range(reach, width_x - reach)]
    acc = dot(inner[0], modes_ref[reach])
    for x in range(1, width_x - 2 * reach):
        acc = acc + dot(inner[x], modes_ref[reach + x])
    p_ref[...] = acc


def side(reach, left, rows, corners, s_ref, taps_ref, bh_ref, bl_ref, eh_ref, el_ref, mix_ref, modes_ref, by_y, mixed):
    width_x, channels, width_y = s_ref.shape
    by = dot2(halves(rows.reshape(reach * channels, width_y)), (bh_ref[...], bl_ref[...]))
    by = by + dot2(halves(corners), (eh_ref[...], el_ref[...]), TN)
    by_y[...] = by.reshape(reach, channels, width_y)
    split = (channels // 8, 8, width_y)
    came = [by_y[left * (reach - 1 - n) + (1 - left) * n].reshape(split) for n in range(reach)]
    taps = [taps_ref[left * d + (1 - left) * (2 * reach - d)][None] for d in range(reach)]
    mix = mix_ref[...]
    for m in range(reach):
        x = left * (reach - 1 - m) + (1 - left) * (width_x - reach + m)
        value = s_ref[x].reshape(split)
        for n in range(m + 1):
            value = value + taps[m - n] * came[n]
        mixed[m] = dot(mix, stacked(value.reshape(channels, width_y))).astype(BF16)
    acc = None
    for m in range(reach):
        term = dot(mixed[m], modes_ref[left * (reach - 1 - m) + (1 - left) * (width_x - reach + m)])
        acc = term if acc is None else acc + term
    return acc


def first_kernel(reach, p_ref, r_ref, core_ref, chip_ref, s_ref, *rest):
    *refs, out_ref, by_y, mixed = rest
    odd = lax.axis_index("gx") % 2
    corners = joined(core_ref[...], chip_ref[...])
    out_ref[...] = p_ref[...] + side(reach, odd, r_ref[...], corners, s_ref, *refs, by_y, mixed)


def second_kernel(reach, owned, p_ref, r_ref, s_ref, *rest):
    *refs, out_ref, by_y, mixed = rest
    odd = lax.axis_index("gx") % 2
    _, channels, width_y = s_ref.shape
    corners = jnp.concatenate([r_ref[reach], jnp.zeros((EDGE - 2 * STRIP, width_y), F32)], axis=0)[:, : reach * channels]
    total = p_ref[...] + side(reach, 1 - odd, r_ref[:reach], corners, s_ref, *refs, by_y, mixed)
    folds = 128 // owned
    rows = channels // folds
    high = out_ref.shape[3]
    for g in range(total.shape[1] // owned):
        piece = jnp.concatenate(
            [total[k * rows : (k + 1) * rows, g * owned : (g + 1) * owned] for k in range(folds)], axis=1
        )
        for k in range(out_ref.shape[0]):
            for j in range(out_ref.shape[2]):
                out_ref[k, g, j] = piece[j * high : (j + 1) * high]


def sum_kernel(parts_ref, coefficients_ref, out_ref):
    channels, owned = out_ref.shape
    _, count, high, lanes = parts_ref.shape
    total = jnp.sum(parts_ref[...], axis=0)
    for k in range(lanes // owned):
        for j in range(count):
            rows = pl.ds((k * count + j) * high, high)
            out_ref[rows] = coefficients_ref[rows] + total[j, :, k * owned : (k + 1) * owned]


def vmem(array):
    return pltpu.with_memory_space_constraint(array, pltpu.VMEM)


def call(body, ins, outs, scratch=(), flops=0, outside=0, keep=True):
    args = [pltpu.with_memory_space_constraint(item, pltpu.HBM) if i < outside else vmem(item) for i, item in enumerate(ins)]
    specs = [pl.BlockSpec(memory_space=pltpu.HBM if i < outside else pltpu.VMEM) for i in range(len(ins))]
    make = pltpu.VMEM if keep else jax.ShapeDtypeStruct
    return pl.pallas_call(
        body,
        out_shape=[make(shape, dtype) for shape, dtype in outs],
        in_specs=specs,
        out_specs=[pl.BlockSpec(memory_space=pltpu.VMEM)] * len(outs),
        scratch_shapes=list(scratch),
        compiler_params=pltpu.CompilerParams(vmem_limit_bytes=24 << 20),
        cost_estimate=pl.CostEstimate(flops=int(1e9), bytes_accessed=1 << 20, transcendentals=0),
    )(*args)


def pairs(count, first):
    found = []
    for low in range(first, count - 1, 2):
        found += [(low, low + 1), (low + 1, low)]
    return found


def local(adjoint_forcing, field_mixing, time_mixing, kernel_east, kernel_north, spatial_modes, coefficients):
    fields, levels, width_x, width_y = adjoint_forcing.shape
    channels, modes, owned = fields * levels, spatial_modes.shape[2], coefficients.shape[0]
    reach = (kernel_east.shape[0] - 1) // 2
    count_x, count_y = lax.axis_size("gx"), lax.axis_size("gy")
    raw = adjoint_forcing.reshape(channels, width_x, width_y)
    slab = (reach, channels, width_y)
    full = ((width_x, channels, width_y), F32)
    t, s1 = call(functools.partial(turn_kernel, reach), [raw], [full, (slab, F32)])
    r1 = lax.ppermute(s1, "gx", pairs(count_x, 0))
    strip = ((STRIP, width_x * channels), F32)
    core, chip = call(functools.partial(strip_kernel, reach), [t], [strip, strip])
    core = lax.ppermute(core, "gy", pairs(count_y, 0))
    chip = lax.ppermute(chip, "gy", pairs(count_y, 1))
    edge = ((EDGE, width_y), BF16)
    band = ((width_y, width_y), BF16)
    wide_rows = -(-channels // 16) * 16
    y, bh, bl, eh, el, along, mix, taps, held = call(
        functools.partial(band_kernel, reach),
        [kernel_east, kernel_north, field_mixing, time_mixing, spatial_modes, t],
        [
            ((channels, width_x, width_y), F32),
            band,
            band,
            edge,
            edge,
            ((width_x, 3 * width_x + -3 * width_x % 96), BF16),
            ((wide_rows, 3 * channels + -3 * channels % 96), BF16),
            ((2 * reach + 1, 8, width_y), F32),
            (spatial_modes.shape, BF16),
        ],
        [
            pltpu.SMEM(kernel_east.shape, F32),
            pltpu.SMEM(kernel_north.shape, F32),
            pltpu.SMEM(field_mixing.shape, F32),
            pltpu.SMEM(time_mixing.shape, F32),
            pltpu.SemaphoreType.DMA((6,)),
        ],
        outside=5,
    )
    (s2,) = call(functools.partial(corner_kernel, reach), [t, core, chip], [((reach + 1, channels, width_y), F32)])
    r2 = lax.ppermute(s2, "gx", pairs(count_x, 1))
    strip = ((STRIP, reach * channels), F32)
    core1, chip1 = call(functools.partial(strip_kernel, reach), [r1], [strip, strip])
    core1 = lax.ppermute(core1, "gy", pairs(count_y, 0))
    chip1 = lax.ppermute(chip1, "gy", pairs(count_y, 1))
    share = ((wide_rows, modes), F32)
    smooth, inner = call(
        functools.partial(tile_kernel, reach),
        [y, core, chip, eh, el, along, mix, held],
        [full, share],
    )
    both = [smooth, taps, bh, bl, eh, el, mix, held]
    room = [pltpu.VMEM(slab, F32), pltpu.VMEM((reach, wide_rows, width_y), BF16)]
    (partial,) = call(
        functools.partial(first_kernel, reach), [inner, r1, core1, chip1, *both], [share], room
    )
    rows = channels * owned // 128
    high = 4 if rows % 4 == 0 else rows
    (out,) = call(
        functools.partial(second_kernel, reach, owned),
        [partial, r2, *both],
        [((count_x, count_y, rows // high, high, 128), F32)],
        room,
    )
    out = out.reshape((count_x * count_y,) + out.shape[2:])
    parts = lax.all_to_all(out, ("gx", "gy"), 0, 0, tiled=True)
    (gradient,) = call(sum_kernel, [parts, coefficients.T], [((channels, owned), F32)], keep=False)
    return gradient.T


def solution(mesh):
    in_specs = (P(None, None, "gx", "gy"), P(), P(), P(), P(), P("gx", "gy", None), P("gy", None))
    out_specs = P("gy", None)
    return jax.shard_map(local, mesh=mesh, in_specs=in_specs, out_specs=out_specs, check_vma=False)
```

```python
import functools

import jax
import jax.numpy as jnp
from jax import lax
from jax.experimental import pallas as pl
from jax.experimental.pallas import tpu as pltpu
from jax.sharding import PartitionSpec as P

F32, BF16 = jnp.float32, jnp.bfloat16
NN = (((1,), (0,)), ((), ()))
NT = (((1,), (1,)), ((), ()))
TN = (((0,), (0,)), ((), ()))
STRIP = 12
ROWS = 4
EDGE = 32
LANES = 128
PITCH = 16


def dot(a, b, dims=NN):
    return lax.dot_general(a, b, dims, preferred_element_type=F32)


def halves(v):
    high = v.astype(BF16)
    return high, (v - high.astype(F32)).astype(BF16)


def dot2(a, b, dims=NN):
    (ah, al), (bh, bl) = a, b
    return dot(ah, bh, dims) + dot(ah, bl, dims) + dot(al, bh, dims)


def iota(shape, dim):
    return lax.broadcasted_iota(jnp.int32, shape, dim)


def stacked(v):
    high = v.astype(BF16).astype(F32)
    parts = [high, v - high, high]
    if (3 * v.shape[0]) % 16:
        parts.append(jnp.zeros((-3 * v.shape[0] % 96, v.shape[1]), F32))
    return jnp.concatenate(parts, axis=0).astype(BF16)


def wide(m):
    high = m.astype(BF16).astype(F32)
    parts = [high, high, m - high]
    if (3 * m.shape[1]) % 16:
        parts.append(jnp.zeros((m.shape[0], -3 * m.shape[1] % 96), F32))
    return jnp.concatenate(parts, axis=1).astype(BF16)


def turn_kernel(reach, a_ref, t_ref, s1_ref):
    t_ref[...] = jnp.swapaxes(a_ref[...], 0, 1)
    odd = lax.axis_index("gx") % 2
    s1_ref[...] = t_ref[pl.ds((1 - odd) * (t_ref.shape[0] - reach), reach)]


def strip_kernel(reach, t_ref, core_ref, chip_ref):
    width_x, channels, width_y = t_ref.shape
    odd = lax.axis_index("gy") % 2
    row, col = iota((EDGE, width_y), 0), iota((EDGE, width_y), 1)
    to_core = row < STRIP
    at = jnp.where(to_core, row, row - STRIP)
    low = jnp.where(to_core, odd, 1 - odd) == 1
    wanted = at + jnp.where(low, 0, width_y - reach)
    pick = jnp.where((col == wanted) & (at < reach), 1.0, 0.0).astype(BF16)
    data = t_ref[...].reshape(width_x * channels, width_y)
    high, rest = halves(data)
    strips = dot(pick, high, NT) + dot(pick, rest, NT)
    for j in range(STRIP // ROWS):
        core_ref[j] = strips[j * ROWS : (j + 1) * ROWS]
        chip_ref[j] = strips[STRIP + j * ROWS : STRIP + (j + 1) * ROWS]


def band_kernel(reach, north_ref, t_ref, y_ref, bh_ref, bl_ref, eh_ref, el_ref, e_ref):
    width_x, channels, width_y = t_ref.shape
    span = 2 * reach + 1
    odd = lax.axis_index("gy") % 2
    shift = iota((width_y, width_y), 0) - iota((width_y, width_y), 1) + reach
    row = iota((EDGE, width_y), 0)
    edge_shifts = []
    for pitch in (STRIP, PITCH):
        from_core = row < pitch
        at = jnp.where(from_core, row, row - pitch)
        left = jnp.where(from_core, odd, 1 - odd) == 1
        source = jnp.where(left, at - reach, width_y + at)
        edge_shifts.append(jnp.where(at < reach, source - iota((EDGE, width_y), 1) + reach, -1))
    first = iota((8, width_y), 1)
    base = jnp.zeros((8, width_y), F32)
    edge = jnp.zeros((EDGE, width_y), F32)
    spread = edge
    for j in range(span):
        tap = north_ref[:, j : j + 1]
        base = jnp.where(first == (reach - j) % width_y, tap, base)
        edge = jnp.where(edge_shifts[0] == j, tap, edge)
        spread = jnp.where(edge_shifts[1] == j, tap, spread)
    e_ref[...] = spread
    rolled = pltpu.roll(jnp.broadcast_to(base[:1], (width_y, width_y)), 0, 1, stride=1, stride_axis=0)
    band = halves(jnp.where((shift >= 0) & (shift < span), rolled, 0.0))
    bh_ref[...], bl_ref[...] = band
    eh_ref[...], el_ref[...] = halves(edge)
    y_ref[...] = dot2(halves(t_ref[...].reshape(width_x * channels, width_y)), band).reshape(t_ref.shape)


def own_kernel(reach, east_ref, field_ref, time_ref, y_ref, s_ref, x_ref, mix_ref, taps_ref):
    width_x, channels, width_y = y_ref.shape
    x_shift = iota((width_x, width_x), 1) - iota((width_x, width_x), 0) + reach
    along = jnp.zeros((width_x, width_x), F32)
    for j in range(2 * reach + 1):
        tap = east_ref[:, j : j + 1]
        along = jnp.where(x_shift == j, tap, along)
        taps_ref[j] = jnp.broadcast_to(tap, taps_ref.shape[1:])
    along = wide(along)
    x_ref[...] = along
    s_ref[...] = along_x(along, y_ref[...])
    fields, levels = field_ref.shape[0], time_ref.shape[0]
    rows = mix_ref.shape[0]
    out, into = iota((rows, channels), 0), iota((rows, channels), 1)
    by_field = jnp.zeros((rows, channels), F32)
    by_time = jnp.zeros((rows, channels), F32)
    for g in range(fields):
        for f in range(fields):
            here = (into // levels == g) & (out // levels == f)
            by_field = jnp.where(here, field_ref[g : g + 1, f : f + 1], by_field)
    for s in range(levels):
        for t in range(levels):
            here = (into % levels == s) & (out % levels == t)
            by_time = jnp.where(here, time_ref[s : s + 1, t : t + 1], by_time)
    mix_ref[...] = wide(by_field * by_time)


def outer_kernel(reach, r_ref, core_ref, chip_ref):
    _, channels, width_y = r_ref.shape
    lane = iota((channels, LANES), 1)
    low = [jnp.zeros((channels, LANES), F32) for _ in range(core_ref.shape[1] // LANES)]
    high = list(low)
    for n in range(reach):
        tile, at = divmod(PITCH * n, LANES)
        first = jnp.where(lane < reach, r_ref[n, :, :LANES], 0.0)
        last = jnp.where(lane >= LANES - reach, r_ref[n, :, width_y - LANES :], 0.0)
        low[tile] += pltpu.roll(first, at, 1) if at else first
        high[tile] += pltpu.roll(last, at + reach, 1)
    odd = lax.axis_index("gy") % 2
    for tile, (a, b) in enumerate(zip(low, high)):
        lanes = slice(tile * LANES, (tile + 1) * LANES)
        core_ref[:, lanes] = jnp.where(odd == 1, a, b)
        chip_ref[:, lanes] = jnp.where(odd == 1, b, a)


def corner_modes_kernel(reach, e_ref, taps_ref, modes_ref, ch_ref, cl_ref, nh_ref, nl_ref, g_ref, h_ref):
    width_x, width_y, modes = modes_ref.shape
    left = lax.axis_index("gx") % 2
    both = jnp.concatenate(halves(e_ref[...]), axis=0)
    half = e_ref.shape[0]
    for m in range(reach):
        g = dot(both, modes_ref[place(reach, left, width_x, m)])
        g_ref[m] = g[:half] + g[half:]
    for n in range(reach):
        value = None
        for m in range(n, reach):
            d = m - n
            tap = taps_ref[left * d + (1 - left) * (2 * reach - d)][None]
            term = tap * g_ref[m].reshape(half // 8, 8, modes)
            value = term if value is None else value + term
        value = value.reshape(half, modes)
        i = left * (reach - 1 - n) + (1 - left) * n
        for side in range(2):
            h_ref[side, i] = value[side * PITCH : (side + 1) * PITCH]
    for side, (high_ref, low_ref) in enumerate(((ch_ref, cl_ref), (nh_ref, nl_ref))):
        high_ref[...], low_ref[...] = halves(h_ref[side].reshape(reach * PITCH, modes))


def joined(core, chip):
    pieces = [piece[j] for piece in (core, chip) for j in range(STRIP // ROWS)]
    return jnp.concatenate(pieces + [jnp.zeros((EDGE - 2 * STRIP, core.shape[2]), F32)], axis=0)


def corner_kernel(reach, y_ref, core_ref, chip_ref, eh_ref, el_ref, before_ref, s2_ref):
    del before_ref
    width_x, channels, width_y = y_ref.shape
    odd = lax.axis_index("gx") % 2
    strips = joined(core_ref[...], chip_ref[...])
    top = strips[:, : reach * channels]
    bottom = strips[:, (width_x - reach) * channels :]
    more = dot2(halves(jnp.where(odd == 1, bottom, top)), (eh_ref[...], el_ref[...]), TN)
    s2_ref[...] = y_ref[pl.ds(odd * (width_x - reach), reach)] + more.reshape(s2_ref.shape)


def along_x(matrix, y):
    by_channel = jnp.swapaxes(y, 0, 1)
    return jnp.swapaxes(jnp.stack([dot(matrix, stacked(by_channel[c])) for c in range(y.shape[1])]), 0, 1)


def tile_kernel(
    reach, own_ref, core_ref, chip_ref, next_ref, eh_ref, el_ref, x_ref, mix_ref, modes_ref, s_ref, p_ref
):
    del next_ref
    width_x, channels, width_y = own_ref.shape
    edge = tuple(ref[:, :LANES] + ref[:, width_y - LANES :] for ref in (eh_ref, el_ref))
    more = dot2(halves(joined(core_ref[...], chip_ref[...])), edge, TN).reshape(width_x, channels, LANES)
    more = along_x(x_ref[...], more)
    left = iota((1, 1, LANES), 2) < LANES // 2
    s_ref[...] = own_ref[...]
    s_ref[:, :, :LANES] += jnp.where(left, more, 0.0)
    s_ref[:, :, width_y - LANES :] += jnp.where(left, 0.0, more)
    mix = mix_ref[...]
    inner = [dot(mix, stacked(s_ref[x])).astype(BF16) for x in range(reach, width_x - reach)]
    acc = dot(inner[0], modes_ref[reach])
    for x in range(1, width_x - 2 * reach):
        acc = acc + dot(inner[x], modes_ref[reach + x])
    p_ref[...] = acc


def place(reach, left, width_x, m):
    return left * (reach - 1 - m) + (1 - left) * (width_x - reach + m)


def added(reach, left, rows, taps_ref, m, count, lanes):
    value = None
    for n in range(m + 1):
        d = m - n
        tap = taps_ref[left * d + (1 - left) * (2 * reach - d), :, :lanes][None]
        term = tap * rows[left * (reach - 1 - n) + (1 - left) * n].reshape(count // 8, 8, lanes)
        value = term if value is None else value + term
    return value.reshape(count, lanes)


def rows_kernel(reach, p_ref, r_ref, bh_ref, bl_ref, s_ref, taps_ref, mix_ref, modes_ref, out_ref, by, mixed):
    left = lax.axis_index("gx") % 2
    rows = dot2(halves(r_ref[...].reshape(-1, r_ref.shape[2])), (bh_ref[...], bl_ref[...]))
    by[...] = rows.reshape(r_ref.shape)
    out_ref[...] = p_ref[...] + side(reach, left, by, s_ref, taps_ref, mix_ref, modes_ref, mixed)


def side(reach, left, rows, s_ref, taps_ref, mix_ref, modes_ref, mixed):
    width_x, channels, width_y = s_ref.shape
    mix = mix_ref[...]
    for m in range(reach):
        value = s_ref[place(reach, left, width_x, m)] + added(reach, left, rows, taps_ref, m, channels, width_y)
        mixed[m] = dot(mix, stacked(value)).astype(BF16)
    total = None
    for m in range(reach):
        term = dot(mixed[m], modes_ref[place(reach, left, width_x, m)])
        total = term if total is None else total + term
    return total


def last_kernel(
    reach, p_ref, r_ref, core_ref, chip_ref, ch_ref, cl_ref, nh_ref, nl_ref, s_ref, taps_ref, mix_ref, modes_ref, out_ref, mixed
):
    odd = lax.axis_index("gx") % 2
    width = ch_ref.shape[0]
    corners = dot2(halves(core_ref[:, :width]), (ch_ref[...], cl_ref[...]))
    corners = corners + dot2(halves(chip_ref[:, :width]), (nh_ref[...], nl_ref[...]))
    total = p_ref[...] + dot(mix_ref[...], stacked(corners))
    total = total + side(reach, 1 - odd, r_ref, s_ref, taps_ref, mix_ref, modes_ref, mixed)
    deliver(total, s_ref.shape[1], out_ref)


def deliver(total, channels, out_ref):
    if len(out_ref.shape) == 2:
        out_ref[...] = total
        return
    _, parts, count, high, lanes = out_ref.shape
    owned = total.shape[1] // parts
    rows = count * high
    for g in range(parts):
        piece = jnp.concatenate(
            [total[k * rows : (k + 1) * rows, g * owned : (g + 1) * owned] for k in range(lanes // owned)], axis=1
        )
        for k in range(out_ref.shape[0]):
            for j in range(count):
                out_ref[k, g, j] = piece[j * high : (j + 1) * high]


def sum_kernel(parts_ref, coefficients_ref, out_ref):
    channels, owned = out_ref.shape
    _, count, high, lanes = parts_ref.shape
    total = jnp.sum(parts_ref[...], axis=0)
    for k in range(lanes // owned):
        for j in range(count):
            rows = pl.ds((k * count + j) * high, high)
            out_ref[rows] = coefficients_ref[rows] + total[j, :, k * owned : (k + 1) * owned]


def vmem(array):
    return pltpu.with_memory_space_constraint(array, pltpu.VMEM)


def call(body, ins, outs, scratch=(), keep=True, weight=1e9):
    args = [vmem(item) for item in ins]
    specs = [pl.BlockSpec(memory_space=pltpu.VMEM)] * len(ins)
    make = pltpu.VMEM if keep else jax.ShapeDtypeStruct
    return pl.pallas_call(
        body,
        out_shape=[make(shape, dtype) for shape, dtype in outs],
        in_specs=specs,
        out_specs=[pl.BlockSpec(memory_space=pltpu.VMEM)] * len(outs),
        scratch_shapes=list(scratch),
        compiler_params=pltpu.CompilerParams(vmem_limit_bytes=24 << 20),
        cost_estimate=pl.CostEstimate(flops=int(weight), bytes_accessed=1 << 20, transcendentals=0),
    )(*args)


def pairs(count, first):
    found = []
    for low in range(first, count - 1, 2):
        found += [(low, low + 1), (low + 1, low)]
    return found


def local(adjoint_forcing, field_mixing, time_mixing, kernel_east, kernel_north, spatial_modes, coefficients):
    fields, levels, width_x, width_y = adjoint_forcing.shape
    channels, modes, owned = fields * levels, spatial_modes.shape[2], coefficients.shape[0]
    reach = (kernel_east.shape[0] - 1) // 2
    count_x, count_y = lax.axis_size("gx"), lax.axis_size("gy")
    raw = adjoint_forcing.reshape(channels, width_x, width_y)
    slab = (reach, channels, width_y)
    full = ((width_x, channels, width_y), F32)
    t, s1 = call(functools.partial(turn_kernel, reach), [raw], [full, (slab, F32)])
    r1 = lax.ppermute(s1, "gx", pairs(count_x, 0))
    strip = ((STRIP // ROWS, ROWS, width_x * channels), F32)
    core, chip = call(functools.partial(strip_kernel, reach), [t], [strip, strip], weight=1e9)
    core = lax.ppermute(core, "gy", pairs(count_y, 0))
    chip = lax.ppermute(chip, "gy", pairs(count_y, 1))
    edge = ((EDGE, width_y), BF16)
    band = ((width_y, width_y), BF16)
    wide_rows = -(-channels // 16) * 16
    y, bh, bl, eh, el, spread = call(
        functools.partial(band_kernel, reach), [kernel_north.reshape(1, -1), t], [full, band, band, edge, edge, ((EDGE, width_y), F32)], weight=1e9)
    own, along, mix, taps = call(
        functools.partial(own_kernel, reach),
        [kernel_east.reshape(1, -1), field_mixing, time_mixing, y],
        [
            full,
            ((width_x, 3 * width_x + -3 * width_x % 96), BF16),
            ((wide_rows, 3 * channels + -3 * channels % 96), BF16),
            ((2 * reach + 1, 8, width_y), F32),
        ], weight=1e9)
    held = vmem(spatial_modes)
    corner = ((reach * PITCH, modes), BF16)
    corner_modes = call(
        functools.partial(corner_modes_kernel, reach),
        [spread, taps, held],
        [corner] * 4,
        [pltpu.VMEM((reach, EDGE, modes), F32), pltpu.VMEM((2, reach, PITCH, modes), F32)],
        weight=1e7,
    )
    (s2,) = call(functools.partial(corner_kernel, reach), [y, core, chip, eh, el, corner_modes[0]], [(slab, F32)], weight=1e7)
    r2 = lax.ppermute(s2, "gx", pairs(count_x, 1))
    strip = ((channels, -(-reach * PITCH // LANES) * LANES), F32)
    core1, chip1 = call(functools.partial(outer_kernel, reach), [r1], [strip, strip], weight=3e8)
    core2 = lax.ppermute(core1, "gy", pairs(count_y, 0))
    chip2 = lax.ppermute(chip1, "gy", pairs(count_y, 1))
    share = ((wide_rows, modes), F32)
    smooth, inner = call(
        functools.partial(tile_kernel, reach),
        [own, core, chip, core1, eh, el, along, mix, held],
        [full, share], weight=1e8)
    both = [smooth, taps, mix, held]
    mixed = pltpu.VMEM((reach, wide_rows, width_y), BF16)
    (partial,) = call(
        functools.partial(rows_kernel, reach),
        [inner, r1, bh, bl, *both],
        [share],
        [pltpu.VMEM(slab, F32), mixed],
        weight=3e8,
    )
    rows = channels * owned // 128
    high = 4 if rows % 4 == 0 else rows
    (out,) = call(
        functools.partial(last_kernel, reach),
        [partial, r2, core2, chip2, *corner_modes, *both],
        [((count_x, count_y, rows // high, high, 128), F32)],
        [mixed],
    )
    out = out.reshape((count_x * count_y,) + out.shape[2:])
    parts = lax.all_to_all(out, ("gx", "gy"), 0, 0, tiled=True)
    (gradient,) = call(sum_kernel, [parts, coefficients.T], [((channels, owned), F32)], keep=False)
    return gradient.T


def solution(mesh):
    in_specs = (P(None, None, "gx", "gy"), P(), P(), P(), P(), P("gx", "gy", None), P("gy", None))
    out_specs = P("gy", None)
    return jax.shard_map(local, mesh=mesh, in_specs=in_specs, out_specs=out_specs, check_vma=False)
```

```python
import functools

import jax
import jax.numpy as jnp
from jax import lax
from jax.experimental import pallas as pl
from jax.experimental.pallas import tpu as pltpu
from jax.sharding import PartitionSpec as P

F32, BF16 = jnp.float32, jnp.bfloat16
NN = (((1,), (0,)), ((), ()))
LANES = 128
PITCH = 16


def dot(a, b, dims=NN):
    return lax.dot_general(a, b, dims, preferred_element_type=F32)


def halves(v):
    high = v.astype(BF16)
    return high, (v - high.astype(F32)).astype(BF16)


def dot2(a, b, dims=NN):
    (ah, al), (bh, bl) = a, b
    return dot(ah, bh, dims) + dot(ah, bl, dims) + dot(al, bh, dims)


def iota(shape, dim):
    return lax.broadcasted_iota(jnp.int32, shape, dim)


def stacked(v):
    high = v.astype(BF16).astype(F32)
    parts = [high, v - high, high]
    if (3 * v.shape[0]) % 16:
        parts.append(jnp.zeros((-3 * v.shape[0] % 96, v.shape[1]), F32))
    return jnp.concatenate(parts, axis=0).astype(BF16)


def wide(m):
    high = m.astype(BF16).astype(F32)
    parts = [high, high, m - high]
    if (3 * m.shape[1]) % 16:
        parts.append(jnp.zeros((m.shape[0], -3 * m.shape[1] % 96), F32))
    return jnp.concatenate(parts, axis=1).astype(BF16)


def turn_kernel(reach, a_hbm, *refs):
    count = (len(refs) - 5) // 2
    small, (t_ref, s1_ref, s2_ref), held, (a_ref, sem) = refs[:count], refs[count : count + 3], refs[count + 3 : -2], refs[-2:]
    copies = [pltpu.make_async_copy(a_hbm, a_ref, sem.at[0])]
    copies += [pltpu.make_async_copy(x, y, sem.at[i + 1]) for i, (x, y) in enumerate(zip(small, held))]
    for copy in copies:
        copy.start()
    for copy in copies:
        copy.wait()
    t_ref[...] = jnp.swapaxes(a_ref[...], 0, 1)
    odd = lax.axis_index("gx") % 2
    far = t_ref.shape[0] - reach
    s1_ref[...] = t_ref[pl.ds((1 - odd) * far, reach)]
    s2_ref[...] = t_ref[pl.ds(odd * far, reach)]


def block_kernel(reach, modes_ref, core_ref, chip_ref):
    width_y = modes_ref.shape[1]
    odd = lax.axis_index("gy") % 2
    low = jnp.swapaxes(modes_ref[:, :PITCH].astype(F32), 0, 1)
    high = jnp.swapaxes(modes_ref[:, width_y - PITCH :].astype(F32), 0, 1)
    for i in range(reach):
        a, b = low[i], high[PITCH - reach + i]
        core_ref[i] = jnp.where(odd == 1, a, b)
        chip_ref[i] = jnp.where(odd == 1, b, a)


def band_kernel(reach, north_ref, t_ref, y_ref, z_ref, bh_ref, bl_ref, ch_ref, cl_ref):
    width_x, channels, width_y = t_ref.shape
    span = 2 * reach + 1
    odd = lax.axis_index("gy") % 2
    shift = iota((width_y, width_y), 0) - iota((width_y, width_y), 1) + reach
    lane = iota((width_y, LANES), 1)
    at = lane % PITCH
    right = jnp.where(lane < PITCH, 1 - odd, odd) == 1
    over = iota((width_y, LANES), 0) - at + jnp.where(right, reach - width_y, 2 * reach)
    over = jnp.where((at < reach) & (lane < 2 * PITCH), over, -1)
    first = iota((8, width_y), 1)
    base = jnp.zeros((8, width_y), F32)
    cross = jnp.zeros((width_y, LANES), F32)
    for j in range(span):
        tap = north_ref[:, j : j + 1]
        base = jnp.where(first == (reach - j) % width_y, tap, base)
        cross = jnp.where(over == j, tap, cross)
    rolled = pltpu.roll(jnp.broadcast_to(base[:1], (width_y, width_y)), 0, 1, stride=1, stride_axis=0)
    band = halves(jnp.where((shift >= 0) & (shift < span), rolled, 0.0))
    cross = halves(cross)
    bh_ref[...], bl_ref[...] = band
    ch_ref[...], cl_ref[...] = cross
    data = halves(t_ref[...].reshape(width_x * channels, width_y))
    y_ref[...] = dot2(data, band).reshape(y_ref.shape)
    z_ref[...] = dot2(data, cross).reshape(z_ref.shape)


def own_kernel(reach, east_ref, field_ref, time_ref, y_ref, z_ref, s_ref, sz_ref, mix_ref, taps_ref):
    width_x, channels, width_y = y_ref.shape
    x_shift = iota((width_x, width_x), 1) - iota((width_x, width_x), 0) + reach
    along = jnp.zeros((width_x, width_x), F32)
    for j in range(2 * reach + 1):
        tap = east_ref[:, j : j + 1]
        along = jnp.where(x_shift == j, tap, along)
        taps_ref[j] = jnp.broadcast_to(tap, taps_ref.shape[1:])
    along = wide(along)
    s_ref[...] = along_x(along, y_ref[...])
    sz_ref[...] = along_x(along, z_ref[...])
    fields, levels = field_ref.shape[0], time_ref.shape[0]
    rows = mix_ref.shape[0]
    out, into = iota((rows, channels), 0), iota((rows, channels), 1)
    by_field = jnp.zeros((rows, channels), F32)
    by_time = jnp.zeros((rows, channels), F32)
    for g in range(fields):
        for f in range(fields):
            here = (into // levels == g) & (out // levels == f)
            by_field = jnp.where(here, field_ref[g : g + 1, f : f + 1], by_field)
    for s in range(levels):
        for t in range(levels):
            here = (into % levels == s) & (out % levels == t)
            by_time = jnp.where(here, time_ref[s : s + 1, t : t + 1], by_time)
    mix_ref[...] = wide(by_field * by_time)


def along_x(matrix, y):
    by_channel = jnp.swapaxes(y, 0, 1)
    return jnp.swapaxes(jnp.stack([dot(matrix, stacked(by_channel[c])) for c in range(y.shape[1])]), 0, 1)


def tile_kernel(reach, s_ref, z_ref, mix_ref, modes_ref, p_ref, l_ref):
    width_x = s_ref.shape[0]
    mix = mix_ref[...]
    inner = [dot(mix, stacked(s_ref[x])).astype(BF16) for x in range(reach, width_x - reach)]
    acc = dot(inner[0], modes_ref[reach])
    for x in range(1, width_x - 2 * reach):
        acc = acc + dot(inner[x], modes_ref[reach + x])
    p_ref[...] = acc
    packed(l_ref, [dot(mix, stacked(z_ref[x])) for x in range(reach, width_x - reach)])


def packed(l_ref, values):
    each = LANES // (2 * PITCH)
    for tile in range(l_ref.shape[1] // LANES):
        total = None
        for k, value in enumerate(values[tile * each : (tile + 1) * each]):
            value = pltpu.roll(value, k * 2 * PITCH, 1) if k else value
            total = value if total is None else total + value
        l_ref[:, tile * LANES : (tile + 1) * LANES] = total


def place(reach, left, width_x, m):
    return left * (reach - 1 - m) + (1 - left) * (width_x - reach + m)


def added(reach, left, rows, taps_ref, m, count, lanes):
    value = None
    for n in range(m + 1):
        d = m - n
        tap = taps_ref[left * d + (1 - left) * (2 * reach - d), :, :lanes][None]
        term = tap * rows[left * (reach - 1 - n) + (1 - left) * n].reshape(count // 8, 8, lanes)
        value = term if value is None else value + term
    return value.reshape(count, lanes)


def side(reach, left, rows, s_ref, taps_ref, mix_ref, modes_ref, mixed):
    width_x, channels, width_y = s_ref.shape
    mix = mix_ref[...]
    for m in range(reach):
        value = s_ref[place(reach, left, width_x, m)] + added(reach, left, rows, taps_ref, m, channels, width_y)
        mixed[m] = dot(mix, stacked(value)).astype(BF16)
    total = None
    for m in range(reach):
        term = dot(mixed[m], modes_ref[place(reach, left, width_x, m)])
        total = term if total is None else total + term
    return total


def smoothed(r_ref, wide_ref, high_ref, low_ref):
    rows = halves(r_ref[...].reshape(-1, r_ref.shape[2]))
    return dot2(rows, (high_ref[...], low_ref[...])).reshape(wide_ref.shape)


def rows_kernel(
    reach, second, p_ref, r_ref, bh_ref, bl_ref, ch_ref, cl_ref, s_ref, z_ref, taps_ref, mix_ref, modes_ref, out_ref, l_ref, by, bz, mixed
):
    width_x, channels, _ = s_ref.shape
    odd = lax.axis_index("gx") % 2
    left = 1 - odd if second else odd
    by[...] = smoothed(r_ref, by, bh_ref, bl_ref)
    bz[...] = smoothed(r_ref, bz, ch_ref, cl_ref)
    mix = mix_ref[...]
    over = []
    for m in range(reach):
        value = z_ref[place(reach, left, width_x, m)] + added(reach, left, bz, taps_ref, m, channels, LANES)
        over.append(dot(mix, stacked(value)))
    over += [jnp.zeros(over[0].shape, F32)] * (-reach % (LANES // (2 * PITCH)))
    packed(l_ref, over)
    out_ref[...] = p_ref[...] + side(reach, left, by, s_ref, taps_ref, mix_ref, modes_ref, mixed)


def gather_kernel(reach, core_ref, chip_ref, out_ref, both):
    _, width_x, modes = core_ref.shape
    odd = lax.axis_index("gx") % 2
    gap = jnp.zeros((PITCH - reach, width_x, modes), F32)
    both[:, :PITCH] = jnp.swapaxes(jnp.concatenate([core_ref[...], gap], axis=0), 0, 1)
    both[:, PITCH:] = jnp.swapaxes(jnp.concatenate([chip_ref[...], gap], axis=0), 0, 1)
    inner = width_x - 2 * reach
    room = -(-reach // (LANES // (2 * PITCH))) * (LANES // (2 * PITCH))
    for x in range(inner):
        out_ref[x] = both[reach + x].astype(BF16)
    for i in range(2):
        left = odd if i == 0 else 1 - odd
        for m in range(room):
            if m < reach:
                out_ref[inner + i * room + m] = both[place(reach, left, width_x, m)].astype(BF16)
            else:
                out_ref[inner + i * room + m] = jnp.zeros(out_ref.shape[1:], BF16)


def over_kernel(reach, p_ref, l0_ref, l1_ref, core_ref, chip_ref, out_ref, blocks_ref, both, blocks):
    gather_kernel(reach, core_ref, chip_ref, blocks, both)
    total = p_ref[...]
    start = 0
    for l_ref in (l0_ref, l1_ref):
        count = l_ref.shape[1] // (2 * PITCH)
        total = total + over(l_ref[...], blocks[start : start + count])
        start += count
    out_ref[...] = total
    blocks_ref[...] = blocks[start:]


def over(rows, blocks):
    value = dot(jnp.concatenate(halves(rows), axis=0), blocks.reshape(-1, blocks.shape[2]))
    half = rows.shape[0]
    return value[:half] + value[half:]


def last_kernel(reach, p_ref, r_ref, blocks_ref, *rest):
    *refs, out_ref, total, l_ref, by, bz, mixed = rest
    rows_kernel(reach, True, p_ref, r_ref, *refs, total, l_ref, by, bz, mixed)
    deliver(total[...] + over(l_ref[...], blocks_ref[...]), r_ref.shape[1], out_ref)


def deliver(total, channels, out_ref):
    if len(out_ref.shape) == 2:
        out_ref[...] = total
        return
    _, parts, count, high, lanes = out_ref.shape
    owned = total.shape[1] // parts
    rows = count * high
    for g in range(parts):
        piece = jnp.concatenate(
            [total[k * rows : (k + 1) * rows, g * owned : (g + 1) * owned] for k in range(lanes // owned)], axis=1
        )
        for k in range(out_ref.shape[0]):
            for j in range(count):
                out_ref[k, g, j] = piece[j * high : (j + 1) * high]


def sum_kernel(parts_ref, coefficients_ref, out_ref):
    channels, owned = out_ref.shape
    _, count, high, lanes = parts_ref.shape
    total = jnp.sum(parts_ref[...], axis=0)
    for k in range(lanes // owned):
        for j in range(count):
            rows = pl.ds((k * count + j) * high, high)
            out_ref[rows] = coefficients_ref[rows] + total[j, :, k * owned : (k + 1) * owned]


def vmem(array):
    return pltpu.with_memory_space_constraint(array, pltpu.VMEM)


def call(body, ins, outs, scratch=(), keep=True, outside=False, weight=1e9):
    place_in = pltpu.HBM if outside else pltpu.VMEM
    make = pltpu.VMEM if keep else jax.ShapeDtypeStruct
    return pl.pallas_call(
        body,
        out_shape=[make(shape, dtype) for shape, dtype in outs],
        in_specs=[pl.BlockSpec(memory_space=place_in)] * len(ins),
        out_specs=[pl.BlockSpec(memory_space=pltpu.VMEM)] * len(outs),
        scratch_shapes=list(scratch),
        compiler_params=pltpu.CompilerParams(vmem_limit_bytes=24 << 20),
        cost_estimate=pl.CostEstimate(flops=int(weight), bytes_accessed=1 << 20, transcendentals=0),
    )(*[pltpu.with_memory_space_constraint(array, place_in) for array in ins])


def pairs(count, first):
    found = []
    for low in range(first, count - 1, 2):
        found += [(low, low + 1), (low + 1, low)]
    return found


def local(adjoint_forcing, field_mixing, time_mixing, kernel_east, kernel_north, spatial_modes, coefficients):
    fields, levels, width_x, width_y = adjoint_forcing.shape
    channels, modes, owned = fields * levels, spatial_modes.shape[2], coefficients.shape[0]
    reach = (kernel_east.shape[0] - 1) // 2
    count_x, count_y = lax.axis_size("gx"), lax.axis_size("gy")
    raw = adjoint_forcing.reshape(channels, width_x, width_y)
    slab = ((reach, channels, width_y), F32)
    full = ((width_x, channels, width_y), F32)
    narrow = ((width_x, channels, LANES), F32)
    band = ((width_y, width_y), BF16)
    cross = ((width_y, LANES), BF16)
    wide_rows = -(-channels // 16) * 16
    share = ((wide_rows, modes), F32)
    each = LANES // (2 * PITCH)
    inner = width_x - 2 * reach
    small = [kernel_north.reshape(1, -1), kernel_east.reshape(1, -1), field_mixing, time_mixing]
    t, s1, s2, *small = call(
        functools.partial(turn_kernel, reach),
        [raw, *small],
        [full, slab, slab] + [(array.shape, F32) for array in small],
        [pltpu.VMEM(raw.shape, F32), pltpu.SemaphoreType.DMA((1 + len(small),))],
        outside=True,
        weight=3e9,
    )
    held = vmem(spatial_modes)
    r1 = lax.ppermute(s1, "gx", pairs(count_x, 0))
    r2 = lax.ppermute(s2, "gx", pairs(count_x, 1))
    y, z, bh, bl, ch, cl = call(
        functools.partial(band_kernel, reach),
        [small[0], t],
        [full, narrow, band, band, cross, cross],
        weight=1e7,
    )
    block = ((reach, width_x, modes), F32)
    core, chip = call(functools.partial(block_kernel, reach), [held], [block, block], weight=3e8)
    core = lax.ppermute(core, "gy", pairs(count_y, 0))
    chip = lax.ppermute(chip, "gy", pairs(count_y, 1))
    s, sz, mix, taps = call(
        functools.partial(own_kernel, reach),
        [*small[1:], y, z],
        [
            full,
            narrow,
            ((wide_rows, 3 * channels + -3 * channels % 96), BF16),
            ((2 * reach + 1, 8, width_y), F32),
        ],
        weight=1e7,
    )
    p, l0 = call(
        functools.partial(tile_kernel, reach),
        [s, sz, mix, held],
        [share, ((wide_rows, inner // each * LANES), F32)],
        weight=1e7,
    )
    both = [bh, bl, ch, cl, s, sz, taps, mix, held]
    layer = (wide_rows, -(-reach // each) * LANES)
    room = [pltpu.VMEM(slab[0], F32), pltpu.VMEM((reach, channels, LANES), F32), pltpu.VMEM((reach, wide_rows, width_y), BF16)]
    p, l1 = call(
        functools.partial(rows_kernel, reach, False), [p, r1, *both], [share, (layer, F32)], room, weight=1e9
    )
    slots = inner + 2 * (layer[1] // (2 * PITCH))
    p, blocks = call(
        functools.partial(over_kernel, reach),
        [p, l0, l1, core, chip],
        [share, ((layer[1] // (2 * PITCH), 2 * PITCH, modes), BF16)],
        [pltpu.VMEM((width_x, 2 * PITCH, modes), F32), pltpu.VMEM((slots, 2 * PITCH, modes), BF16)],
        weight=1e7,
    )
    rows = channels * owned // 128
    high = 4 if rows % 4 == 0 else rows
    (out,) = call(
        functools.partial(last_kernel, reach),
        [p, r2, blocks, *both],
        [((count_x, count_y, rows // high, high, 128), F32)],
        [pltpu.VMEM(share[0], F32), pltpu.VMEM(layer, F32), *room],
    )
    out = out.reshape((count_x * count_y,) + out.shape[2:])
    parts = lax.all_to_all(out, ("gx", "gy"), 0, 0, tiled=True)
    (gradient,) = call(sum_kernel, [parts, coefficients.T], [((channels, owned), F32)], keep=False)
    return gradient.T


def solution(mesh):
    in_specs = (P(None, None, "gx", "gy"), P(), P(), P(), P(), P("gx", "gy", None), P("gy", None))
    out_specs = P("gy", None)
    return jax.shard_map(local, mesh=mesh, in_specs=in_specs, out_specs=out_specs, check_vma=False)
```

```python
import functools

import jax
import jax.numpy as jnp
from jax import lax
from jax.experimental import pallas as pl
from jax.experimental.pallas import tpu as pltpu
from jax.sharding import PartitionSpec as P

F32, BF16 = jnp.float32, jnp.bfloat16
NN = (((1,), (0,)), ((), ()))
LANES = 128
PITCH = 16


def dot(a, b, dims=NN):
    return lax.dot_general(a, b, dims, preferred_element_type=F32)


def halves(v):
    high = v.astype(BF16)
    return high, (v - high.astype(F32)).astype(BF16)


def dot2(a, b, dims=NN):
    (ah, al), (bh, bl) = a, b
    return dot(ah, bh, dims) + dot(ah, bl, dims) + dot(al, bh, dims)


def iota(shape, dim):
    return lax.broadcasted_iota(jnp.int32, shape, dim)


def stacked(v):
    high = v.astype(BF16).astype(F32)
    parts = [high, v - high, high]
    if (3 * v.shape[0]) % 16:
        parts.append(jnp.zeros((-3 * v.shape[0] % 96, v.shape[1]), F32))
    return jnp.concatenate(parts, axis=0).astype(BF16)


def wide(m):
    high = m.astype(BF16).astype(F32)
    parts = [high, high, m - high]
    if (3 * m.shape[1]) % 16:
        parts.append(jnp.zeros((m.shape[0], -3 * m.shape[1] % 96), F32))
    return jnp.concatenate(parts, axis=1).astype(BF16)


def first_kernel(reach, a_hbm, modes_hbm, *refs):
    count = (len(refs) - 5) // 2
    small, s1_ref, ends, held = refs[:count], refs[count], refs[count + 1 : count + 3], refs[count + 3 : -2]
    rows_ref, sem = refs[-2:]
    window, width_x, width_y = rows_ref.shape[1], a_hbm.shape[1], a_hbm.shape[2]
    odd = lax.axis_index("gx") % 2
    start = pl.multiple_of((1 - odd) * (width_x - window), 8)
    pairs_of = [(a_hbm.at[:, pl.ds(start, window)], rows_ref)]
    pairs_of += [(modes_hbm.at[:, pl.ds(i * (width_y - PITCH), PITCH)], ends[i]) for i in range(2)]
    pairs_of += list(zip(small, held))
    copies = [pltpu.make_async_copy(x, y, sem.at[i]) for i, (x, y) in enumerate(pairs_of)]
    for copy in copies:
        copy.start()
    for copy in copies:
        copy.wait()
    rows = jnp.swapaxes(rows_ref[...], 0, 1)
    s1_ref[...] = jnp.where(odd == 1, rows[:reach], rows[window - reach :])


def turn_kernel(reach, a_ref, before_ref, t_ref, s2_ref):
    del before_ref
    t_ref[...] = jnp.swapaxes(a_ref[...], 0, 1)
    s2_ref[...] = t_ref[pl.ds(lax.axis_index("gx") % 2 * (t_ref.shape[0] - reach), reach)]


def block_kernel(reach, low_ref, high_ref, core_ref, chip_ref):
    odd = lax.axis_index("gy") % 2
    low = jnp.swapaxes(low_ref[...].astype(F32), 0, 1)
    high = jnp.swapaxes(high_ref[...].astype(F32), 0, 1)
    for i in range(reach):
        a, b = low[i], high[PITCH - reach + i]
        core_ref[i] = jnp.where(odd == 1, a, b)
        chip_ref[i] = jnp.where(odd == 1, b, a)


def band_kernel(reach, north_ref, t_ref, y_ref, z_ref, bh_ref, bl_ref, ch_ref, cl_ref):
    width_x, channels, width_y = t_ref.shape
    span = 2 * reach + 1
    odd = lax.axis_index("gy") % 2
    shift = iota((width_y, width_y), 0) - iota((width_y, width_y), 1) + reach
    lane = iota((width_y, LANES), 1)
    at = lane % PITCH
    right = jnp.where(lane < PITCH, 1 - odd, odd) == 1
    over = iota((width_y, LANES), 0) - at + jnp.where(right, reach - width_y, 2 * reach)
    over = jnp.where((at < reach) & (lane < 2 * PITCH), over, -1)
    first = iota((8, width_y), 1)
    base = jnp.zeros((8, width_y), F32)
    cross = jnp.zeros((width_y, LANES), F32)
    for j in range(span):
        tap = north_ref[:, j : j + 1]
        base = jnp.where(first == (reach - j) % width_y, tap, base)
        cross = jnp.where(over == j, tap, cross)
    rolled = pltpu.roll(jnp.broadcast_to(base[:1], (width_y, width_y)), 0, 1, stride=1, stride_axis=0)
    band = halves(jnp.where((shift >= 0) & (shift < span), rolled, 0.0))
    cross = halves(cross)
    bh_ref[...], bl_ref[...] = band
    ch_ref[...], cl_ref[...] = cross
    data = halves(t_ref[...].reshape(width_x * channels, width_y))
    y_ref[...] = dot2(data, band).reshape(y_ref.shape)
    z_ref[...] = dot2(data, cross).reshape(z_ref.shape)


def own_kernel(reach, east_ref, field_ref, time_ref, y_ref, z_ref, s_ref, sz_ref, mix_ref, taps_ref):
    width_x, channels, width_y = y_ref.shape
    x_shift = iota((width_x, width_x), 1) - iota((width_x, width_x), 0) + reach
    along = jnp.zeros((width_x, width_x), F32)
    for j in range(2 * reach + 1):
        tap = east_ref[:, j : j + 1]
        along = jnp.where(x_shift == j, tap, along)
        taps_ref[j] = jnp.broadcast_to(tap, taps_ref.shape[1:])
    along = wide(along)
    s_ref[...] = along_x(along, y_ref[...])
    sz_ref[...] = along_x(along, z_ref[...])
    fields, levels = field_ref.shape[0], time_ref.shape[0]
    rows = mix_ref.shape[0]
    out, into = iota((rows, channels), 0), iota((rows, channels), 1)
    by_field = jnp.zeros((rows, channels), F32)
    by_time = jnp.zeros((rows, channels), F32)
    for g in range(fields):
        for f in range(fields):
            here = (into // levels == g) & (out // levels == f)
            by_field = jnp.where(here, field_ref[g : g + 1, f : f + 1], by_field)
    for s in range(levels):
        for t in range(levels):
            here = (into % levels == s) & (out % levels == t)
            by_time = jnp.where(here, time_ref[s : s + 1, t : t + 1], by_time)
    mix_ref[...] = wide(by_field * by_time)


def along_x(matrix, y):
    by_channel = jnp.swapaxes(y, 0, 1)
    return jnp.swapaxes(jnp.stack([dot(matrix, stacked(by_channel[c])) for c in range(y.shape[1])]), 0, 1)


def tile_kernel(reach, s_ref, z_ref, mix_ref, modes_ref, p_ref, l_ref):
    width_x = s_ref.shape[0]
    mix = mix_ref[...]
    inner = [dot(mix, stacked(s_ref[x])).astype(BF16) for x in range(reach, width_x - reach)]
    acc = dot(inner[0], modes_ref[reach])
    for x in range(1, width_x - 2 * reach):
        acc = acc + dot(inner[x], modes_ref[reach + x])
    p_ref[...] = acc
    packed(l_ref, [z_ref[x] for x in range(reach, width_x - reach)])


def packed(l_ref, values):
    each = LANES // (2 * PITCH)
    for tile in range(l_ref.shape[1] // LANES):
        total = None
        for k, value in enumerate(values[tile * each : (tile + 1) * each]):
            value = pltpu.roll(value, k * 2 * PITCH, 1) if k else value
            total = value if total is None else total + value
        l_ref[:, tile * LANES : (tile + 1) * LANES] = total


def place(reach, left, width_x, m):
    return left * (reach - 1 - m) + (1 - left) * (width_x - reach + m)


def added(reach, left, rows, taps_ref, m, count, lanes):
    value = None
    for n in range(m + 1):
        d = m - n
        tap = taps_ref[left * d + (1 - left) * (2 * reach - d), :, :lanes][None]
        term = tap * rows[left * (reach - 1 - n) + (1 - left) * n].reshape(count // 8, 8, lanes)
        value = term if value is None else value + term
    return value.reshape(count, lanes)


def side(reach, left, rows, s_ref, taps_ref, mix_ref, modes_ref, mixed):
    width_x, channels, width_y = s_ref.shape
    mix = mix_ref[...]
    for m in range(reach):
        value = s_ref[place(reach, left, width_x, m)] + added(reach, left, rows, taps_ref, m, channels, width_y)
        mixed[m] = dot(mix, stacked(value)).astype(BF16)
    total = None
    for m in range(reach):
        term = dot(mixed[m], modes_ref[place(reach, left, width_x, m)])
        total = term if total is None else total + term
    return total


def smoothed(r_ref, wide_ref, high_ref, low_ref):
    rows = halves(r_ref[...].reshape(-1, r_ref.shape[2]))
    return dot2(rows, (high_ref[...], low_ref[...])).reshape(wide_ref.shape)


def rows_kernel(
    reach, second, p_ref, r_ref, bh_ref, bl_ref, ch_ref, cl_ref, s_ref, z_ref, taps_ref, mix_ref, modes_ref, out_ref, l_ref, by, bz, mixed
):
    width_x, channels, _ = s_ref.shape
    odd = lax.axis_index("gx") % 2
    left = 1 - odd if second else odd
    by[...] = smoothed(r_ref, by, bh_ref, bl_ref)
    bz[...] = smoothed(r_ref, bz, ch_ref, cl_ref)
    over = []
    for m in range(reach):
        over.append(z_ref[place(reach, left, width_x, m)] + added(reach, left, bz, taps_ref, m, channels, LANES))
    over += [jnp.zeros(over[0].shape, F32)] * (-reach % (LANES // (2 * PITCH)))
    packed(l_ref, over)
    out_ref[...] = p_ref[...] + side(reach, left, by, s_ref, taps_ref, mix_ref, modes_ref, mixed)


def gather_kernel(reach, core_ref, chip_ref, out_ref, both):
    _, width_x, modes = core_ref.shape
    odd = lax.axis_index("gx") % 2
    gap = jnp.zeros((PITCH - reach, width_x, modes), F32)
    both[:, :PITCH] = jnp.swapaxes(jnp.concatenate([core_ref[...], gap], axis=0), 0, 1)
    both[:, PITCH:] = jnp.swapaxes(jnp.concatenate([chip_ref[...], gap], axis=0), 0, 1)
    inner = width_x - 2 * reach
    room = -(-reach // (LANES // (2 * PITCH))) * (LANES // (2 * PITCH))
    for x in range(inner):
        out_ref[x] = both[reach + x].astype(BF16)
    for i in range(2):
        left = odd if i == 0 else 1 - odd
        for m in range(room):
            if m < reach:
                out_ref[inner + i * room + m] = both[place(reach, left, width_x, m)].astype(BF16)
            else:
                out_ref[inner + i * room + m] = jnp.zeros(out_ref.shape[1:], BF16)


def over_kernel(reach, l0_ref, l1_ref, core_ref, chip_ref, out_ref, blocks_ref, both, blocks):
    gather_kernel(reach, core_ref, chip_ref, blocks, both)
    start = 0
    total = None
    for l_ref in (l0_ref, l1_ref):
        count = l_ref.shape[1] // (2 * PITCH)
        value = over(l_ref[...], blocks[start : start + count])
        total = value if total is None else total + value
        start += count
    out_ref[...] = total
    blocks_ref[...] = blocks[start:]


def over(rows, blocks):
    high = rows.astype(BF16).astype(F32)
    value = dot(jnp.concatenate([high, rows - high], axis=0).astype(BF16), blocks.reshape(-1, blocks.shape[2]))
    half = rows.shape[0]
    return value[:half] + value[half:]


def last_kernel(reach, p_ref, r_ref, o_ref, blocks_ref, *rest):
    *refs, out_ref, total, l_ref, by, bz, mixed = rest
    rows_kernel(reach, True, p_ref, r_ref, *refs, total, l_ref, by, bz, mixed)
    ends = o_ref[...] + over(l_ref[...], blocks_ref[...])
    deliver(total[...] + dot(refs[7][...], stacked(ends)), r_ref.shape[1], out_ref)


def deliver(total, channels, out_ref):
    if len(out_ref.shape) == 2:
        out_ref[...] = total
        return
    _, parts, count, high, lanes = out_ref.shape
    owned = total.shape[1] // parts
    rows = count * high
    for g in range(parts):
        piece = jnp.concatenate(
            [total[k * rows : (k + 1) * rows, g * owned : (g + 1) * owned] for k in range(lanes // owned)], axis=1
        )
        for k in range(out_ref.shape[0]):
            for j in range(count):
                out_ref[k, g, j] = piece[j * high : (j + 1) * high]


def sum_kernel(parts_ref, coefficients_ref, out_ref):
    channels, owned = out_ref.shape
    _, count, high, lanes = parts_ref.shape
    total = jnp.sum(parts_ref[...], axis=0)
    for k in range(lanes // owned):
        for j in range(count):
            rows = pl.ds((k * count + j) * high, high)
            out_ref[rows] = coefficients_ref[rows] + total[j, :, k * owned : (k + 1) * owned]


def vmem(array):
    return pltpu.with_memory_space_constraint(array, pltpu.VMEM)


def call(body, ins, outs, scratch=(), keep=True, outside=False, weight=1e9):
    place_in = pltpu.HBM if outside else pltpu.VMEM
    make = pltpu.VMEM if keep else jax.ShapeDtypeStruct
    return pl.pallas_call(
        body,
        out_shape=[make(shape, dtype) for shape, dtype in outs],
        in_specs=[pl.BlockSpec(memory_space=place_in)] * len(ins),
        out_specs=[pl.BlockSpec(memory_space=pltpu.VMEM)] * len(outs),
        scratch_shapes=list(scratch),
        compiler_params=pltpu.CompilerParams(vmem_limit_bytes=24 << 20),
        cost_estimate=pl.CostEstimate(flops=int(weight), bytes_accessed=1 << 20, transcendentals=0),
    )(*[pltpu.with_memory_space_constraint(array, place_in) for array in ins])


def pairs(count, first):
    found = []
    for low in range(first, count - 1, 2):
        found += [(low, low + 1), (low + 1, low)]
    return found


def local(adjoint_forcing, field_mixing, time_mixing, kernel_east, kernel_north, spatial_modes, coefficients):
    fields, levels, width_x, width_y = adjoint_forcing.shape
    channels, modes, owned = fields * levels, spatial_modes.shape[2], coefficients.shape[0]
    reach = (kernel_east.shape[0] - 1) // 2
    count_x, count_y = lax.axis_size("gx"), lax.axis_size("gy")
    raw = adjoint_forcing.reshape(channels, width_x, width_y)
    slab = ((reach, channels, width_y), F32)
    full = ((width_x, channels, width_y), F32)
    narrow = ((width_x, channels, LANES), F32)
    band = ((width_y, width_y), BF16)
    cross = ((width_y, LANES), BF16)
    wide_rows = -(-channels // 16) * 16
    share = ((wide_rows, modes), F32)
    each = LANES // (2 * PITCH)
    inner = width_x - 2 * reach
    small = [kernel_north.reshape(1, -1), kernel_east.reshape(1, -1), field_mixing, time_mixing]
    s1, low, high, *small = call(
        functools.partial(first_kernel, reach),
        [raw, spatial_modes, *small],
        [slab] + [((width_x, PITCH, modes), BF16)] * 2 + [(array.shape, F32) for array in small],
        [pltpu.VMEM((channels, -(-reach // 8) * 8, width_y), F32), pltpu.SemaphoreType.DMA((3 + len(small),))],
        outside=True,
        weight=3e8,
    )
    t, s2 = call(functools.partial(turn_kernel, reach), [raw, s1], [full, slab], weight=3e9)
    held = vmem(spatial_modes)
    r1 = lax.ppermute(s1, "gx", pairs(count_x, 0))
    r2 = lax.ppermute(s2, "gx", pairs(count_x, 1))
    y, z, bh, bl, ch, cl = call(
        functools.partial(band_kernel, reach),
        [small[0], t],
        [full, narrow, band, band, cross, cross],
        weight=1e9,
    )
    block = ((reach, width_x, modes), F32)
    core, chip = call(functools.partial(block_kernel, reach), [low, high], [block, block], weight=3e8)
    core = lax.ppermute(core, "gy", pairs(count_y, 0))
    chip = lax.ppermute(chip, "gy", pairs(count_y, 1))
    s, sz, mix, taps = call(
        functools.partial(own_kernel, reach),
        [*small[1:], y, z],
        [
            full,
            narrow,
            ((wide_rows, 3 * channels + -3 * channels % 96), BF16),
            ((2 * reach + 1, 8, width_y), F32),
        ],
        weight=1e7,
    )
    p, l0 = call(
        functools.partial(tile_kernel, reach),
        [s, sz, mix, held],
        [share, ((channels, inner // each * LANES), F32)],
        weight=1e7,
    )
    both = [bh, bl, ch, cl, s, sz, taps, mix, held]
    layer = (channels, -(-reach // each) * LANES)
    room = [pltpu.VMEM(slab[0], F32), pltpu.VMEM((reach, channels, LANES), F32), pltpu.VMEM((reach, wide_rows, width_y), BF16)]
    p, l1 = call(
        functools.partial(rows_kernel, reach, False), [p, r1, *both], [share, (layer, F32)], room, weight=1e9
    )
    slots = inner + 2 * (layer[1] // (2 * PITCH))
    ends, blocks = call(
        functools.partial(over_kernel, reach),
        [l0, l1, core, chip],
        [((channels, modes), F32), ((layer[1] // (2 * PITCH), 2 * PITCH, modes), BF16)],
        [pltpu.VMEM((width_x, 2 * PITCH, modes), F32), pltpu.VMEM((slots, 2 * PITCH, modes), BF16)],
        weight=1e7,
    )
    rows = channels * owned // 128
    high = 4 if rows % 4 == 0 else rows
    (out,) = call(
        functools.partial(last_kernel, reach),
        [p, r2, ends, blocks, *both],
        [((count_x, count_y, rows // high, high, 128), F32)],
        [pltpu.VMEM(share[0], F32), pltpu.VMEM(layer, F32), *room],
    )
    out = out.reshape((count_x * count_y,) + out.shape[2:])
    parts = lax.all_to_all(out, ("gx", "gy"), 0, 0, tiled=True)
    (gradient,) = call(sum_kernel, [parts, coefficients.T], [((channels, owned), F32)], keep=False)
    return gradient.T


def solution(mesh):
    in_specs = (P(None, None, "gx", "gy"), P(), P(), P(), P(), P("gx", "gy", None), P("gy", None))
    out_specs = P("gy", None)
    return jax.shard_map(local, mesh=mesh, in_specs=in_specs, out_specs=out_specs, check_vma=False)
```

```python
import functools

import jax
import jax.numpy as jnp
from jax import lax
from jax.experimental import pallas as pl
from jax.experimental.pallas import tpu as pltpu
from jax.sharding import PartitionSpec as P

F32, BF16 = jnp.float32, jnp.bfloat16
NN = (((1,), (0,)), ((), ()))
LANES = 128
PITCH = 16


def dot(a, b, dims=NN):
    return lax.dot_general(a, b, dims, preferred_element_type=F32)


def halves(v):
    high = v.astype(BF16)
    return high, (v - high.astype(F32)).astype(BF16)


def dot2(a, b, dims=NN):
    (ah, al), (bh, bl) = a, b
    return dot(ah, bh, dims) + dot(ah, bl, dims) + dot(al, bh, dims)


def iota(shape, dim):
    return lax.broadcasted_iota(jnp.int32, shape, dim)


def stacked(v):
    high = v.astype(BF16).astype(F32)
    parts = [high, v - high, high]
    if (3 * v.shape[0]) % 16:
        parts.append(jnp.zeros((-3 * v.shape[0] % 96, v.shape[1]), F32))
    return jnp.concatenate(parts, axis=0).astype(BF16)


def wide(m):
    high = m.astype(BF16).astype(F32)
    parts = [high, high, m - high]
    if (3 * m.shape[1]) % 16:
        parts.append(jnp.zeros((m.shape[0], -3 * m.shape[1] % 96), F32))
    return jnp.concatenate(parts, axis=1).astype(BF16)


def first_kernel(reach, a_hbm, *refs):
    count = (len(refs) - 3) // 2
    small, s1_ref, held, (rows_ref, sem) = refs[:count], refs[count], refs[count + 1 : -2], refs[-2:]
    window, width_x = rows_ref.shape[1], a_hbm.shape[1]
    odd = lax.axis_index("gx") % 2
    start = pl.multiple_of((1 - odd) * (width_x - window), 8)
    copies = [pltpu.make_async_copy(a_hbm.at[:, pl.ds(start, window)], rows_ref, sem.at[0])]
    copies += [pltpu.make_async_copy(x, y, sem.at[i + 1]) for i, (x, y) in enumerate(zip(small, held))]
    for copy in copies:
        copy.start()
    for copy in copies:
        copy.wait()
    rows = jnp.swapaxes(rows_ref[...], 0, 1)
    s1_ref[...] = jnp.where(odd == 1, rows[:reach], rows[window - reach :])


def turn_kernel(reach, a_ref, before_ref, t_ref, s2_ref):
    del before_ref
    t_ref[...] = jnp.swapaxes(a_ref[...], 0, 1)
    s2_ref[...] = t_ref[pl.ds(lax.axis_index("gx") % 2 * (t_ref.shape[0] - reach), reach)]


def block_kernel(reach, modes_ref, core_ref, chip_ref):
    width_y = modes_ref.shape[1]
    odd = lax.axis_index("gy") % 2
    low = jnp.swapaxes(modes_ref[:, :PITCH].astype(F32), 0, 1)
    high = jnp.swapaxes(modes_ref[:, width_y - PITCH :].astype(F32), 0, 1)
    for i in range(reach):
        a, b = low[i], high[PITCH - reach + i]
        core_ref[i] = jnp.where(odd == 1, a, b)
        chip_ref[i] = jnp.where(odd == 1, b, a)


def band_kernel(reach, north_ref, t_ref, y_ref, z_ref, bh_ref, bl_ref, ch_ref, cl_ref):
    width_x, channels, width_y = t_ref.shape
    span = 2 * reach + 1
    odd = lax.axis_index("gy") % 2
    shift = iota((width_y, width_y), 0) - iota((width_y, width_y), 1) + reach
    lane = iota((width_y, LANES), 1)
    at = lane % PITCH
    right = jnp.where(lane < PITCH, 1 - odd, odd) == 1
    over = iota((width_y, LANES), 0) - at + jnp.where(right, reach - width_y, 2 * reach)
    over = jnp.where((at < reach) & (lane < 2 * PITCH), over, -1)
    first = iota((8, width_y), 1)
    base = jnp.zeros((8, width_y), F32)
    cross = jnp.zeros((width_y, LANES), F32)
    for j in range(span):
        tap = north_ref[:, j : j + 1]
        base = jnp.where(first == (reach - j) % width_y, tap, base)
        cross = jnp.where(over == j, tap, cross)
    rolled = pltpu.roll(jnp.broadcast_to(base[:1], (width_y, width_y)), 0, 1, stride=1, stride_axis=0)
    band = halves(jnp.where((shift >= 0) & (shift < span), rolled, 0.0))
    cross = halves(cross)
    bh_ref[...], bl_ref[...] = band
    ch_ref[...], cl_ref[...] = cross
    data = halves(t_ref[...].reshape(width_x * channels, width_y))
    y_ref[...] = dot2(data, band).reshape(y_ref.shape)
    z_ref[...] = dot2(data, cross).reshape(z_ref.shape)


def own_kernel(reach, east_ref, field_ref, time_ref, y_ref, z_ref, s_ref, sz_ref, mix_ref, taps_ref):
    width_x, channels, width_y = y_ref.shape
    x_shift = iota((width_x, width_x), 1) - iota((width_x, width_x), 0) + reach
    along = jnp.zeros((width_x, width_x), F32)
    for j in range(2 * reach + 1):
        tap = east_ref[:, j : j + 1]
        along = jnp.where(x_shift == j, tap, along)
        taps_ref[j] = jnp.broadcast_to(tap, taps_ref.shape[1:])
    along = wide(along)
    s_ref[...] = along_x(along, y_ref[...])
    sz_ref[...] = along_x(along, z_ref[...])
    fields, levels = field_ref.shape[0], time_ref.shape[0]
    rows = mix_ref.shape[0]
    out, into = iota((rows, channels), 0), iota((rows, channels), 1)
    by_field = jnp.zeros((rows, channels), F32)
    by_time = jnp.zeros((rows, channels), F32)
    for g in range(fields):
        for f in range(fields):
            here = (into // levels == g) & (out // levels == f)
            by_field = jnp.where(here, field_ref[g : g + 1, f : f + 1], by_field)
    for s in range(levels):
        for t in range(levels):
            here = (into % levels == s) & (out % levels == t)
            by_time = jnp.where(here, time_ref[s : s + 1, t : t + 1], by_time)
    mix_ref[...] = wide(by_field * by_time)


def along_x(matrix, y):
    by_channel = jnp.swapaxes(y, 0, 1)
    return jnp.swapaxes(jnp.stack([dot(matrix, stacked(by_channel[c])) for c in range(y.shape[1])]), 0, 1)


def tile_kernel(reach, s_ref, z_ref, mix_ref, modes_ref, p_ref, l_ref):
    width_x = s_ref.shape[0]
    mix = mix_ref[...]
    inner = [dot(mix, stacked(s_ref[x])).astype(BF16) for x in range(reach, width_x - reach)]
    acc = dot(inner[0], modes_ref[reach])
    for x in range(1, width_x - 2 * reach):
        acc = acc + dot(inner[x], modes_ref[reach + x])
    p_ref[...] = acc
    packed(l_ref, [z_ref[x] for x in range(reach, width_x - reach)])


def packed(l_ref, values):
    each = LANES // (2 * PITCH)
    for tile in range(l_ref.shape[1] // LANES):
        total = None
        for k, value in enumerate(values[tile * each : (tile + 1) * each]):
            value = pltpu.roll(value, k * 2 * PITCH, 1) if k else value
            total = value if total is None else total + value
        l_ref[:, tile * LANES : (tile + 1) * LANES] = total


def place(reach, left, width_x, m):
    return left * (reach - 1 - m) + (1 - left) * (width_x - reach + m)


def added(reach, left, rows, taps_ref, m, count, lanes):
    value = None
    for n in range(m + 1):
        d = m - n
        tap = taps_ref[left * d + (1 - left) * (2 * reach - d), :, :lanes][None]
        term = tap * rows[left * (reach - 1 - n) + (1 - left) * n].reshape(count // 8, 8, lanes)
        value = term if value is None else value + term
    return value.reshape(count, lanes)


def side(reach, left, rows, s_ref, taps_ref, mix_ref, modes_ref, mixed):
    width_x, channels, width_y = s_ref.shape
    mix = mix_ref[...]
    for m in range(reach):
        value = s_ref[place(reach, left, width_x, m)] + added(reach, left, rows, taps_ref, m, channels, width_y)
        mixed[m] = dot(mix, stacked(value)).astype(BF16)
    total = None
    for m in range(reach):
        term = dot(mixed[m], modes_ref[place(reach, left, width_x, m)])
        total = term if total is None else total + term
    return total


def smoothed(r_ref, wide_ref, high_ref, low_ref):
    rows = halves(r_ref[...].reshape(-1, r_ref.shape[2]))
    return dot2(rows, (high_ref[...], low_ref[...])).reshape(wide_ref.shape)


def rows_kernel(
    reach, second, p_ref, r_ref, bh_ref, bl_ref, ch_ref, cl_ref, s_ref, z_ref, taps_ref, mix_ref, modes_ref, out_ref, l_ref, by, bz, mixed
):
    width_x, channels, _ = s_ref.shape
    odd = lax.axis_index("gx") % 2
    left = 1 - odd if second else odd
    by[...] = smoothed(r_ref, by, bh_ref, bl_ref)
    bz[...] = smoothed(r_ref, bz, ch_ref, cl_ref)
    over = []
    for m in range(reach):
        over.append(z_ref[place(reach, left, width_x, m)] + added(reach, left, bz, taps_ref, m, channels, LANES))
    over += [jnp.zeros(over[0].shape, F32)] * (-reach % (LANES // (2 * PITCH)))
    packed(l_ref, over)
    out_ref[...] = p_ref[...] + side(reach, left, by, s_ref, taps_ref, mix_ref, modes_ref, mixed)


def gather_kernel(reach, core_ref, chip_ref, out_ref, both):
    _, width_x, modes = core_ref.shape
    odd = lax.axis_index("gx") % 2
    gap = jnp.zeros((PITCH - reach, width_x, modes), F32)
    both[:, :PITCH] = jnp.swapaxes(jnp.concatenate([core_ref[...], gap], axis=0), 0, 1)
    both[:, PITCH:] = jnp.swapaxes(jnp.concatenate([chip_ref[...], gap], axis=0), 0, 1)
    inner = width_x - 2 * reach
    room = -(-reach // (LANES // (2 * PITCH))) * (LANES // (2 * PITCH))
    for x in range(inner):
        out_ref[x] = both[reach + x].astype(BF16)
    for i in range(2):
        left = odd if i == 0 else 1 - odd
        for m in range(room):
            if m < reach:
                out_ref[inner + i * room + m] = both[place(reach, left, width_x, m)].astype(BF16)
            else:
                out_ref[inner + i * room + m] = jnp.zeros(out_ref.shape[1:], BF16)


def over_kernel(reach, l0_ref, l1_ref, core_ref, chip_ref, out_ref, blocks_ref, both, blocks):
    gather_kernel(reach, core_ref, chip_ref, blocks, both)
    start = 0
    total = None
    for l_ref in (l0_ref, l1_ref):
        count = l_ref.shape[1] // (2 * PITCH)
        value = over(l_ref[...], blocks[start : start + count])
        total = value if total is None else total + value
        start += count
    out_ref[...] = total
    blocks_ref[...] = blocks[start:]


def over(rows, blocks):
    high = rows.astype(BF16).astype(F32)
    value = dot(jnp.concatenate([high, rows - high], axis=0).astype(BF16), blocks.reshape(-1, blocks.shape[2]))
    half = rows.shape[0]
    return value[:half] + value[half:]


def last_kernel(reach, p_ref, r_ref, o_ref, blocks_ref, *rest):
    *refs, out_ref, total, l_ref, by, bz, mixed = rest
    rows_kernel(reach, True, p_ref, r_ref, *refs, total, l_ref, by, bz, mixed)
    ends = o_ref[...] + over(l_ref[...], blocks_ref[...])
    deliver(total[...] + dot(refs[7][...], stacked(ends)), r_ref.shape[1], out_ref)


def deliver(total, channels, out_ref):
    if len(out_ref.shape) == 2:
        out_ref[...] = total
        return
    _, parts, count, high, lanes = out_ref.shape
    owned = total.shape[1] // parts
    rows = count * high
    for g in range(parts):
        piece = jnp.concatenate(
            [total[k * rows : (k + 1) * rows, g * owned : (g + 1) * owned] for k in range(lanes // owned)], axis=1
        )
        for k in range(out_ref.shape[0]):
            for j in range(count):
                out_ref[k, g, j] = piece[j * high : (j + 1) * high]


def sum_kernel(parts_ref, coefficients_ref, out_ref):
    channels, owned = out_ref.shape
    _, count, high, lanes = parts_ref.shape
    total = jnp.sum(parts_ref[...], axis=0)
    for k in range(lanes // owned):
        for j in range(count):
            rows = pl.ds((k * count + j) * high, high)
            out_ref[rows] = coefficients_ref[rows] + total[j, :, k * owned : (k + 1) * owned]


def vmem(array):
    return pltpu.with_memory_space_constraint(array, pltpu.VMEM)


def call(body, ins, outs, scratch=(), keep=True, outside=False, weight=1e9):
    place_in = pltpu.HBM if outside else pltpu.VMEM
    make = pltpu.VMEM if keep else jax.ShapeDtypeStruct
    return pl.pallas_call(
        body,
        out_shape=[make(shape, dtype) for shape, dtype in outs],
        in_specs=[pl.BlockSpec(memory_space=place_in)] * len(ins),
        out_specs=[pl.BlockSpec(memory_space=pltpu.VMEM)] * len(outs),
        scratch_shapes=list(scratch),
        compiler_params=pltpu.CompilerParams(vmem_limit_bytes=24 << 20),
        cost_estimate=pl.CostEstimate(flops=int(weight), bytes_accessed=1 << 20, transcendentals=0),
    )(*[pltpu.with_memory_space_constraint(array, place_in) for array in ins])


def pairs(count, first):
    found = []
    for low in range(first, count - 1, 2):
        found += [(low, low + 1), (low + 1, low)]
    return found


def local(adjoint_forcing, field_mixing, time_mixing, kernel_east, kernel_north, spatial_modes, coefficients):
    fields, levels, width_x, width_y = adjoint_forcing.shape
    channels, modes, owned = fields * levels, spatial_modes.shape[2], coefficients.shape[0]
    reach = (kernel_east.shape[0] - 1) // 2
    count_x, count_y = lax.axis_size("gx"), lax.axis_size("gy")
    raw = adjoint_forcing.reshape(channels, width_x, width_y)
    slab = ((reach, channels, width_y), F32)
    full = ((width_x, channels, width_y), F32)
    narrow = ((width_x, channels, LANES), F32)
    band = ((width_y, width_y), BF16)
    cross = ((width_y, LANES), BF16)
    wide_rows = -(-channels // 16) * 16
    share = ((wide_rows, modes), F32)
    each = LANES // (2 * PITCH)
    inner = width_x - 2 * reach
    small = [kernel_north.reshape(1, -1), kernel_east.reshape(1, -1), field_mixing, time_mixing]
    s1, *small = call(
        functools.partial(first_kernel, reach),
        [raw, *small],
        [slab] + [(array.shape, F32) for array in small],
        [pltpu.VMEM((channels, -(-reach // 8) * 8, width_y), F32), pltpu.SemaphoreType.DMA((1 + len(small),))],
        outside=True,
        weight=3e9,
    )
    t, s2 = call(functools.partial(turn_kernel, reach), [raw, s1], [full, slab], weight=1e7)
    held = vmem(spatial_modes)
    r1 = lax.ppermute(s1, "gx", pairs(count_x, 0))
    r2 = lax.ppermute(s2, "gx", pairs(count_x, 1))
    y, z, bh, bl, ch, cl = call(
        functools.partial(band_kernel, reach),
        [small[0], t],
        [full, narrow, band, band, cross, cross],
        weight=1e7,
    )
    block = ((reach, width_x, modes), F32)
    core, chip = call(functools.partial(block_kernel, reach), [held], [block, block], weight=3e8)
    core = lax.ppermute(core, "gy", pairs(count_y, 0))
    chip = lax.ppermute(chip, "gy", pairs(count_y, 1))
    s, sz, mix, taps = call(
        functools.partial(own_kernel, reach),
        [*small[1:], y, z],
        [
            full,
            narrow,
            ((wide_rows, 3 * channels + -3 * channels % 96), BF16),
            ((2 * reach + 1, 8, width_y), F32),
        ],
        weight=1e7,
    )
    p, l0 = call(
        functools.partial(tile_kernel, reach),
        [s, sz, mix, held],
        [share, ((channels, inner // each * LANES), F32)],
        weight=1e7,
    )
    both = [bh, bl, ch, cl, s, sz, taps, mix, held]
    layer = (channels, -(-reach // each) * LANES)
    room = [pltpu.VMEM(slab[0], F32), pltpu.VMEM((reach, channels, LANES), F32), pltpu.VMEM((reach, wide_rows, width_y), BF16)]
    p, l1 = call(
        functools.partial(rows_kernel, reach, False), [p, r1, *both], [share, (layer, F32)], room, weight=1e9
    )
    slots = inner + 2 * (layer[1] // (2 * PITCH))
    ends, blocks = call(
        functools.partial(over_kernel, reach),
        [l0, l1, core, chip],
        [((channels, modes), F32), ((layer[1] // (2 * PITCH), 2 * PITCH, modes), BF16)],
        [pltpu.VMEM((width_x, 2 * PITCH, modes), F32), pltpu.VMEM((slots, 2 * PITCH, modes), BF16)],
        weight=1e7,
    )
    rows = channels * owned // 128
    high = 4 if rows % 4 == 0 else rows
    (out,) = call(
        functools.partial(last_kernel, reach),
        [p, r2, ends, blocks, *both],
        [((count_x, count_y, rows // high, high, 128), F32)],
        [pltpu.VMEM(share[0], F32), pltpu.VMEM(layer, F32), *room],
    )
    out = out.reshape((count_x * count_y,) + out.shape[2:])
    parts = lax.all_to_all(out, ("gx", "gy"), 0, 0, tiled=True)
    (gradient,) = call(sum_kernel, [parts, coefficients.T], [((channels, owned), F32)], keep=False)
    return gradient.T


def solution(mesh):
    in_specs = (P(None, None, "gx", "gy"), P(), P(), P(), P(), P("gx", "gy", None), P("gy", None))
    out_specs = P("gy", None)
    return jax.shard_map(local, mesh=mesh, in_specs=in_specs, out_specs=out_specs, check_vma=False)
```

```python
import functools

import jax
import jax.numpy as jnp
from jax import lax
from jax.experimental import pallas as pl
from jax.experimental.pallas import tpu as pltpu
from jax.sharding import PartitionSpec as P

F32, BF16 = jnp.float32, jnp.bfloat16
NN = (((1,), (0,)), ((), ()))
LANES = 128
PITCH = 16


def dot(a, b, dims=NN):
    return lax.dot_general(a, b, dims, preferred_element_type=F32)


def halves(v):
    high = v.astype(BF16)
    return high, (v - high.astype(F32)).astype(BF16)


def dot2(a, b, dims=NN):
    (ah, al), (bh, bl) = a, b
    return dot(ah, bh, dims) + dot(ah, bl, dims) + dot(al, bh, dims)


def iota(shape, dim):
    return lax.broadcasted_iota(jnp.int32, shape, dim)


def stacked(v):
    high = v.astype(BF16).astype(F32)
    parts = [high, v - high, high]
    if (3 * v.shape[0]) % 16:
        parts.append(jnp.zeros((-3 * v.shape[0] % 96, v.shape[1]), F32))
    return jnp.concatenate(parts, axis=0).astype(BF16)


def wide(m):
    high = m.astype(BF16).astype(F32)
    parts = [high, high, m - high]
    if (3 * m.shape[1]) % 16:
        parts.append(jnp.zeros((m.shape[0], -3 * m.shape[1] % 96), F32))
    return jnp.concatenate(parts, axis=1).astype(BF16)


def first_kernel(reach, a_hbm, *refs):
    count = (len(refs) - 2) // 2
    small, s1_ref, held, sem = refs[:count], refs[count], refs[count + 1 : -1], refs[-1]
    odd = lax.axis_index("gx") % 2
    far = a_hbm.shape[1] - reach
    copies = [pltpu.make_async_copy(x, y, sem.at[i]) for i, (x, y) in enumerate(zip(small, held))]

    def rows(start):
        return [pltpu.make_async_copy(a_hbm.at[:, start + n], s1_ref.at[n], sem.at[count + n]) for n in range(reach)]

    for left in range(2):

        @pl.when(odd == left)
        def _():
            for copy in rows((1 - left) * far):
                copy.start()

    for copy in copies:
        copy.start()
    for left in range(2):

        @pl.when(odd == left)
        def _():
            for copy in rows((1 - left) * far):
                copy.wait()

    for copy in copies:
        copy.wait()


def turn_kernel(reach, a_ref, before_ref, t_ref, s2_ref):
    del before_ref
    t_ref[...] = jnp.swapaxes(a_ref[...], 0, 1)
    s2_ref[...] = t_ref[pl.ds(lax.axis_index("gx") % 2 * (t_ref.shape[0] - reach), reach)]


def block_kernel(reach, modes_ref, core_ref, chip_ref):
    width_y = modes_ref.shape[1]
    odd = lax.axis_index("gy") % 2
    low = jnp.swapaxes(modes_ref[:, :PITCH].astype(F32), 0, 1)
    high = jnp.swapaxes(modes_ref[:, width_y - PITCH :].astype(F32), 0, 1)
    for i in range(reach):
        a, b = low[i], high[PITCH - reach + i]
        core_ref[i] = jnp.where(odd == 1, a, b)
        chip_ref[i] = jnp.where(odd == 1, b, a)


def band_kernel(reach, north_ref, t_ref, y_ref, z_ref, bh_ref, bl_ref, ch_ref, cl_ref):
    width_x, channels, width_y = t_ref.shape
    span = 2 * reach + 1
    odd = lax.axis_index("gy") % 2
    shift = iota((width_y, width_y), 0) - iota((width_y, width_y), 1) + reach
    lane = iota((width_y, LANES), 1)
    at = lane % PITCH
    right = jnp.where(lane < PITCH, 1 - odd, odd) == 1
    over = iota((width_y, LANES), 0) - at + jnp.where(right, reach - width_y, 2 * reach)
    over = jnp.where((at < reach) & (lane < 2 * PITCH), over, -1)
    first = iota((8, width_y), 1)
    base = jnp.zeros((8, width_y), F32)
    cross = jnp.zeros((width_y, LANES), F32)
    for j in range(span):
        tap = north_ref[:, j : j + 1]
        base = jnp.where(first == (reach - j) % width_y, tap, base)
        cross = jnp.where(over == j, tap, cross)
    rolled = pltpu.roll(jnp.broadcast_to(base[:1], (width_y, width_y)), 0, 1, stride=1, stride_axis=0)
    band = halves(jnp.where((shift >= 0) & (shift < span), rolled, 0.0))
    cross = halves(cross)
    bh_ref[...], bl_ref[...] = band
    ch_ref[...], cl_ref[...] = cross
    data = halves(t_ref[...].reshape(width_x * channels, width_y))
    y_ref[...] = dot2(data, band).reshape(y_ref.shape)
    z_ref[...] = dot2(data, cross).reshape(z_ref.shape)


def own_kernel(reach, east_ref, field_ref, time_ref, y_ref, z_ref, s_ref, sz_ref, mix_ref, taps_ref):
    width_x, channels, width_y = y_ref.shape
    x_shift = iota((width_x, width_x), 1) - iota((width_x, width_x), 0) + reach
    along = jnp.zeros((width_x, width_x), F32)
    for j in range(2 * reach + 1):
        tap = east_ref[:, j : j + 1]
        along = jnp.where(x_shift == j, tap, along)
        taps_ref[j] = jnp.broadcast_to(tap, taps_ref.shape[1:])
    along = wide(along)
    s_ref[...] = along_x(along, y_ref[...])
    sz_ref[...] = along_x(along, z_ref[...])
    fields, levels = field_ref.shape[0], time_ref.shape[0]
    rows = mix_ref.shape[0]
    out, into = iota((rows, channels), 0), iota((rows, channels), 1)
    by_field = jnp.zeros((rows, channels), F32)
    by_time = jnp.zeros((rows, channels), F32)
    for g in range(fields):
        for f in range(fields):
            here = (into // levels == g) & (out // levels == f)
            by_field = jnp.where(here, field_ref[g : g + 1, f : f + 1], by_field)
    for s in range(levels):
        for t in range(levels):
            here = (into % levels == s) & (out % levels == t)
            by_time = jnp.where(here, time_ref[s : s + 1, t : t + 1], by_time)
    mix_ref[...] = wide(by_field * by_time)


def along_x(matrix, y):
    by_channel = jnp.swapaxes(y, 0, 1)
    return jnp.swapaxes(jnp.stack([dot(matrix, stacked(by_channel[c])) for c in range(y.shape[1])]), 0, 1)


def tile_kernel(reach, s_ref, z_ref, mix_ref, modes_ref, p_ref, l_ref):
    width_x = s_ref.shape[0]
    mix = mix_ref[...]
    inner = [dot(mix, stacked(s_ref[x])).astype(BF16) for x in range(reach, width_x - reach)]
    acc = dot(inner[0], modes_ref[reach])
    for x in range(1, width_x - 2 * reach):
        acc = acc + dot(inner[x], modes_ref[reach + x])
    p_ref[...] = acc
    packed(l_ref, [z_ref[x] for x in range(reach, width_x - reach)])


def packed(l_ref, values):
    each = LANES // (2 * PITCH)
    for tile in range(l_ref.shape[1] // LANES):
        total = None
        for k, value in enumerate(values[tile * each : (tile + 1) * each]):
            value = pltpu.roll(value, k * 2 * PITCH, 1) if k else value
            total = value if total is None else total + value
        l_ref[:, tile * LANES : (tile + 1) * LANES] = total


def place(reach, left, width_x, m):
    return left * (reach - 1 - m) + (1 - left) * (width_x - reach + m)


def added(reach, left, rows, taps_ref, m, count, lanes):
    value = None
    for n in range(m + 1):
        d = m - n
        tap = taps_ref[left * d + (1 - left) * (2 * reach - d), :, :lanes][None]
        term = tap * rows[left * (reach - 1 - n) + (1 - left) * n].reshape(count // 8, 8, lanes)
        value = term if value is None else value + term
    return value.reshape(count, lanes)


def side(reach, left, rows, s_ref, taps_ref, mix_ref, modes_ref, mixed):
    width_x, channels, width_y = s_ref.shape
    mix = mix_ref[...]
    for m in range(reach):
        value = s_ref[place(reach, left, width_x, m)] + added(reach, left, rows, taps_ref, m, channels, width_y)
        mixed[m] = dot(mix, stacked(value)).astype(BF16)
    total = None
    for m in range(reach):
        term = dot(mixed[m], modes_ref[place(reach, left, width_x, m)])
        total = term if total is None else total + term
    return total


def smoothed(r_ref, wide_ref, high_ref, low_ref):
    rows = halves(r_ref[...].reshape(-1, r_ref.shape[2]))
    return dot2(rows, (high_ref[...], low_ref[...])).reshape(wide_ref.shape)


def rows_kernel(
    reach, second, p_ref, r_ref, bh_ref, bl_ref, ch_ref, cl_ref, s_ref, z_ref, taps_ref, mix_ref, modes_ref, out_ref, l_ref, by, bz, mixed
):
    width_x, channels, _ = s_ref.shape
    odd = lax.axis_index("gx") % 2
    left = 1 - odd if second else odd
    by[...] = smoothed(r_ref, by, bh_ref, bl_ref)
    bz[...] = smoothed(r_ref, bz, ch_ref, cl_ref)
    over = []
    for m in range(reach):
        over.append(z_ref[place(reach, left, width_x, m)] + added(reach, left, bz, taps_ref, m, channels, LANES))
    over += [jnp.zeros(over[0].shape, F32)] * (-reach % (LANES // (2 * PITCH)))
    packed(l_ref, over)
    out_ref[...] = p_ref[...] + side(reach, left, by, s_ref, taps_ref, mix_ref, modes_ref, mixed)


def gather_kernel(reach, core_ref, chip_ref, out_ref, both):
    _, width_x, modes = core_ref.shape
    odd = lax.axis_index("gx") % 2
    gap = jnp.zeros((PITCH - reach, width_x, modes), F32)
    both[:, :PITCH] = jnp.swapaxes(jnp.concatenate([core_ref[...], gap], axis=0), 0, 1)
    both[:, PITCH:] = jnp.swapaxes(jnp.concatenate([chip_ref[...], gap], axis=0), 0, 1)
    inner = width_x - 2 * reach
    room = -(-reach // (LANES // (2 * PITCH))) * (LANES // (2 * PITCH))
    for x in range(inner):
        out_ref[x] = both[reach + x].astype(BF16)
    for i in range(2):
        left = odd if i == 0 else 1 - odd
        for m in range(room):
            if m < reach:
                out_ref[inner + i * room + m] = both[place(reach, left, width_x, m)].astype(BF16)
            else:
                out_ref[inner + i * room + m] = jnp.zeros(out_ref.shape[1:], BF16)


def over_kernel(reach, l0_ref, l1_ref, core_ref, chip_ref, out_ref, blocks_ref, both, blocks):
    gather_kernel(reach, core_ref, chip_ref, blocks, both)
    start = 0
    total = None
    for l_ref in (l0_ref, l1_ref):
        count = l_ref.shape[1] // (2 * PITCH)
        value = over(l_ref[...], blocks[start : start + count])
        total = value if total is None else total + value
        start += count
    out_ref[...] = total
    blocks_ref[...] = blocks[start:]


def over(rows, blocks):
    high = rows.astype(BF16).astype(F32)
    value = dot(jnp.concatenate([high, rows - high], axis=0).astype(BF16), blocks.reshape(-1, blocks.shape[2]))
    half = rows.shape[0]
    return value[:half] + value[half:]


def last_kernel(reach, p_ref, r_ref, o_ref, blocks_ref, *rest):
    *refs, out_ref, total, l_ref, by, bz, mixed = rest
    rows_kernel(reach, True, p_ref, r_ref, *refs, total, l_ref, by, bz, mixed)
    ends = o_ref[...] + over(l_ref[...], blocks_ref[...])
    deliver(total[...] + dot(refs[7][...], stacked(ends)), r_ref.shape[1], out_ref)


def deliver(total, channels, out_ref):
    if len(out_ref.shape) == 2:
        out_ref[...] = total
        return
    _, parts, count, high, lanes = out_ref.shape
    owned = total.shape[1] // parts
    rows = count * high
    for g in range(parts):
        piece = jnp.concatenate(
            [total[k * rows : (k + 1) * rows, g * owned : (g + 1) * owned] for k in range(lanes // owned)], axis=1
        )
        for k in range(out_ref.shape[0]):
            for j in range(count):
                out_ref[k, g, j] = piece[j * high : (j + 1) * high]


def sum_kernel(parts_ref, coefficients_ref, out_ref):
    channels, owned = out_ref.shape
    _, count, high, lanes = parts_ref.shape
    total = jnp.sum(parts_ref[...], axis=0)
    for k in range(lanes // owned):
        for j in range(count):
            rows = pl.ds((k * count + j) * high, high)
            out_ref[rows] = coefficients_ref[rows] + total[j, :, k * owned : (k + 1) * owned]


def vmem(array):
    return pltpu.with_memory_space_constraint(array, pltpu.VMEM)


def call(body, ins, outs, scratch=(), keep=True, outside=False, weight=1e9):
    place_in = pltpu.HBM if outside else pltpu.VMEM
    make = pltpu.VMEM if keep else jax.ShapeDtypeStruct
    return pl.pallas_call(
        body,
        out_shape=[make(shape, dtype) for shape, dtype in outs],
        in_specs=[pl.BlockSpec(memory_space=place_in)] * len(ins),
        out_specs=[pl.BlockSpec(memory_space=pltpu.VMEM)] * len(outs),
        scratch_shapes=list(scratch),
        compiler_params=pltpu.CompilerParams(vmem_limit_bytes=24 << 20),
        cost_estimate=pl.CostEstimate(flops=int(weight), bytes_accessed=1 << 20, transcendentals=0),
    )(*[pltpu.with_memory_space_constraint(array, place_in) for array in ins])


def pairs(count, first):
    found = []
    for low in range(first, count - 1, 2):
        found += [(low, low + 1), (low + 1, low)]
    return found


def local(adjoint_forcing, field_mixing, time_mixing, kernel_east, kernel_north, spatial_modes, coefficients):
    fields, levels, width_x, width_y = adjoint_forcing.shape
    channels, modes, owned = fields * levels, spatial_modes.shape[2], coefficients.shape[0]
    reach = (kernel_east.shape[0] - 1) // 2
    count_x, count_y = lax.axis_size("gx"), lax.axis_size("gy")
    raw = adjoint_forcing.reshape(channels, width_x, width_y)
    slab = ((reach, channels, width_y), F32)
    full = ((width_x, channels, width_y), F32)
    narrow = ((width_x, channels, LANES), F32)
    band = ((width_y, width_y), BF16)
    cross = ((width_y, LANES), BF16)
    wide_rows = -(-channels // 16) * 16
    share = ((wide_rows, modes), F32)
    each = LANES // (2 * PITCH)
    inner = width_x - 2 * reach
    small = [kernel_north.reshape(1, -1), kernel_east.reshape(1, -1), field_mixing, time_mixing]
    s1, *small = call(
        functools.partial(first_kernel, reach),
        [raw, *small],
        [slab] + [(array.shape, F32) for array in small],
        [pltpu.SemaphoreType.DMA((reach + len(small),))],
        outside=True,
        weight=3e9,
    )
    t, s2 = call(functools.partial(turn_kernel, reach), [raw, s1], [full, slab], weight=1e7)
    held = vmem(spatial_modes)
    r1 = lax.ppermute(s1, "gx", pairs(count_x, 0))
    r2 = lax.ppermute(s2, "gx", pairs(count_x, 1))
    y, z, bh, bl, ch, cl = call(
        functools.partial(band_kernel, reach),
        [small[0], t],
        [full, narrow, band, band, cross, cross],
        weight=1e7,
    )
    block = ((reach, width_x, modes), F32)
    core, chip = call(functools.partial(block_kernel, reach), [held], [block, block], weight=3e8)
    core = lax.ppermute(core, "gy", pairs(count_y, 0))
    chip = lax.ppermute(chip, "gy", pairs(count_y, 1))
    s, sz, mix, taps = call(
        functools.partial(own_kernel, reach),
        [*small[1:], y, z],
        [
            full,
            narrow,
            ((wide_rows, 3 * channels + -3 * channels % 96), BF16),
            ((2 * reach + 1, 8, width_y), F32),
        ],
        weight=1e7,
    )
    p, l0 = call(
        functools.partial(tile_kernel, reach),
        [s, sz, mix, held],
        [share, ((channels, inner // each * LANES), F32)],
        weight=1e7,
    )
    both = [bh, bl, ch, cl, s, sz, taps, mix, held]
    layer = (channels, -(-reach // each) * LANES)
    room = [pltpu.VMEM(slab[0], F32), pltpu.VMEM((reach, channels, LANES), F32), pltpu.VMEM((reach, wide_rows, width_y), BF16)]
    p, l1 = call(
        functools.partial(rows_kernel, reach, False), [p, r1, *both], [share, (layer, F32)], room, weight=1e9
    )
    slots = inner + 2 * (layer[1] // (2 * PITCH))
    ends, blocks = call(
        functools.partial(over_kernel, reach),
        [l0, l1, core, chip],
        [((channels, modes), F32), ((layer[1] // (2 * PITCH), 2 * PITCH, modes), BF16)],
        [pltpu.VMEM((width_x, 2 * PITCH, modes), F32), pltpu.VMEM((slots, 2 * PITCH, modes), BF16)],
        weight=1e7,
    )
    rows = channels * owned // 128
    high = 4 if rows % 4 == 0 else rows
    (out,) = call(
        functools.partial(last_kernel, reach),
        [p, r2, ends, blocks, *both],
        [((count_x, count_y, rows // high, high, 128), F32)],
        [pltpu.VMEM(share[0], F32), pltpu.VMEM(layer, F32), *room],
    )
    out = out.reshape((count_x * count_y,) + out.shape[2:])
    parts = lax.all_to_all(out, ("gx", "gy"), 0, 0, tiled=True)
    (gradient,) = call(sum_kernel, [parts, coefficients.T], [((channels, owned), F32)], keep=False)
    return gradient.T


def solution(mesh):
    in_specs = (P(None, None, "gx", "gy"), P(), P(), P(), P(), P("gx", "gy", None), P("gy", None))
    out_specs = P("gy", None)
    return jax.shard_map(local, mesh=mesh, in_specs=in_specs, out_specs=out_specs, check_vma=False)
```

```python
import functools

import jax
import jax.numpy as jnp
from jax import lax
from jax.experimental import pallas as pl
from jax.experimental.pallas import tpu as pltpu
from jax.sharding import PartitionSpec as P

F32, BF16 = jnp.float32, jnp.bfloat16
NN = (((1,), (0,)), ((), ()))
LANES = 128
PITCH = 16


def dot(a, b, dims=NN):
    return lax.dot_general(a, b, dims, preferred_element_type=F32)


def halves(v):
    high = v.astype(BF16)
    return high, (v - high.astype(F32)).astype(BF16)


def dot2(a, b, dims=NN):
    (ah, al), (bh, bl) = a, b
    return dot(ah, bh, dims) + dot(ah, bl, dims) + dot(al, bh, dims)


def iota(shape, dim):
    return lax.broadcasted_iota(jnp.int32, shape, dim)


def stacked(v):
    high = v.astype(BF16).astype(F32)
    parts = [high, v - high, high]
    if (3 * v.shape[0]) % 16:
        parts.append(jnp.zeros((-3 * v.shape[0] % 96, v.shape[1]), F32))
    return jnp.concatenate(parts, axis=0).astype(BF16)


def wide(m):
    high = m.astype(BF16).astype(F32)
    parts = [high, high, m - high]
    if (3 * m.shape[1]) % 16:
        parts.append(jnp.zeros((m.shape[0], -3 * m.shape[1] % 96), F32))
    return jnp.concatenate(parts, axis=1).astype(BF16)


def first_kernel(reach, a_hbm, *refs):
    count = (len(refs) - 2) // 2
    small, s1_ref, held, sem = refs[:count], refs[count], refs[count + 1 : -1], refs[-1]
    odd = lax.axis_index("gx") % 2
    far = a_hbm.shape[1] - reach
    copies = [pltpu.make_async_copy(x, y, sem.at[i]) for i, (x, y) in enumerate(zip(small, held))]

    def rows(start):
        return [pltpu.make_async_copy(a_hbm.at[:, start + n], s1_ref.at[n], sem.at[count + n]) for n in range(reach)]

    for left in range(2):

        @pl.when(odd == left)
        def _():
            for copy in rows((1 - left) * far):
                copy.start()

    for copy in copies:
        copy.start()
    for left in range(2):

        @pl.when(odd == left)
        def _():
            for copy in rows((1 - left) * far):
                copy.wait()

    for copy in copies:
        copy.wait()


def turn_kernel(reach, a_ref, before_ref, t_ref, s2_ref):
    del before_ref
    t_ref[...] = jnp.swapaxes(a_ref[...], 0, 1)
    s2_ref[...] = t_ref[pl.ds(lax.axis_index("gx") % 2 * (t_ref.shape[0] - reach), reach)]


def block_kernel(reach, modes_ref, core_ref, chip_ref):
    width_y = modes_ref.shape[1]
    odd = lax.axis_index("gy") % 2
    low = jnp.swapaxes(modes_ref[:, :PITCH].astype(F32), 0, 1)
    high = jnp.swapaxes(modes_ref[:, width_y - PITCH :].astype(F32), 0, 1)
    for i in range(reach):
        a, b = low[i], high[PITCH - reach + i]
        core_ref[i] = jnp.where(odd == 1, a, b)
        chip_ref[i] = jnp.where(odd == 1, b, a)


def band_kernel(reach, north_ref, t_ref, y_ref, z_ref, bh_ref, bl_ref, ch_ref, cl_ref):
    width_x, channels, width_y = t_ref.shape
    span = 2 * reach + 1
    odd = lax.axis_index("gy") % 2
    shift = iota((width_y, width_y), 0) - iota((width_y, width_y), 1) + reach
    lane = iota((width_y, LANES), 1)
    at = lane % PITCH
    right = jnp.where(lane < PITCH, 1 - odd, odd) == 1
    over = iota((width_y, LANES), 0) - at + jnp.where(right, reach - width_y, 2 * reach)
    over = jnp.where((at < reach) & (lane < 2 * PITCH), over, -1)
    first = iota((8, width_y), 1)
    base = jnp.zeros((8, width_y), F32)
    cross = jnp.zeros((width_y, LANES), F32)
    for j in range(span):
        tap = north_ref[:, j : j + 1]
        base = jnp.where(first == (reach - j) % width_y, tap, base)
        cross = jnp.where(over == j, tap, cross)
    rolled = pltpu.roll(jnp.broadcast_to(base[:1], (width_y, width_y)), 0, 1, stride=1, stride_axis=0)
    band = halves(jnp.where((shift >= 0) & (shift < span), rolled, 0.0))
    cross = halves(cross)
    bh_ref[...], bl_ref[...] = band
    ch_ref[...], cl_ref[...] = cross
    data = halves(t_ref[...].reshape(width_x * channels, width_y))
    y_ref[...] = dot2(data, band).reshape(y_ref.shape)
    z_ref[...] = dot2(data, cross).reshape(z_ref.shape)


def own_kernel(reach, east_ref, field_ref, time_ref, y_ref, z_ref, s_ref, sz_ref, mix_ref, taps_ref):
    width_x, channels, width_y = y_ref.shape
    x_shift = iota((width_x, width_x), 1) - iota((width_x, width_x), 0) + reach
    along = jnp.zeros((width_x, width_x), F32)
    for j in range(2 * reach + 1):
        tap = east_ref[:, j : j + 1]
        along = jnp.where(x_shift == j, tap, along)
        taps_ref[j] = jnp.broadcast_to(tap, taps_ref.shape[1:])
    along = wide(along)
    s_ref[...] = along_x(along, y_ref[...])
    sz_ref[...] = along_x(along, z_ref[...])
    fields, levels = field_ref.shape[0], time_ref.shape[0]
    rows = mix_ref.shape[0]
    out, into = iota((rows, channels), 0), iota((rows, channels), 1)
    by_field = jnp.zeros((rows, channels), F32)
    by_time = jnp.zeros((rows, channels), F32)
    for g in range(fields):
        for f in range(fields):
            here = (into // levels == g) & (out // levels == f)
            by_field = jnp.where(here, field_ref[g : g + 1, f : f + 1], by_field)
    for s in range(levels):
        for t in range(levels):
            here = (into % levels == s) & (out % levels == t)
            by_time = jnp.where(here, time_ref[s : s + 1, t : t + 1], by_time)
    mix_ref[...] = wide(by_field * by_time)


def along_x(matrix, y):
    by_channel = jnp.swapaxes(y, 0, 1)
    return jnp.swapaxes(jnp.stack([dot(matrix, stacked(by_channel[c])) for c in range(y.shape[1])]), 0, 1)


def tile_kernel(reach, s_ref, z_ref, mix_ref, modes_ref, p_ref, l_ref):
    width_x = s_ref.shape[0]
    mix = mix_ref[...]
    inner = [dot(mix, stacked(s_ref[x])).astype(BF16) for x in range(reach, width_x - reach)]
    acc = dot(inner[0], modes_ref[reach])
    for x in range(1, width_x - 2 * reach):
        acc = acc + dot(inner[x], modes_ref[reach + x])
    p_ref[...] = acc
    packed(l_ref, [z_ref[x] for x in range(reach, width_x - reach)])


def packed(l_ref, values):
    each = LANES // (2 * PITCH)
    for tile in range(l_ref.shape[1] // LANES):
        total = None
        for k, value in enumerate(values[tile * each : (tile + 1) * each]):
            value = pltpu.roll(value, k * 2 * PITCH, 1) if k else value
            total = value if total is None else total + value
        l_ref[:, tile * LANES : (tile + 1) * LANES] = total


def place(reach, left, width_x, m):
    return left * (reach - 1 - m) + (1 - left) * (width_x - reach + m)


def added(reach, left, rows, taps_ref, m, count, lanes):
    value = None
    for n in range(m + 1):
        d = m - n
        tap = taps_ref[left * d + (1 - left) * (2 * reach - d), :, :lanes][None]
        term = tap * rows[left * (reach - 1 - n) + (1 - left) * n].reshape(count // 8, 8, lanes)
        value = term if value is None else value + term
    return value.reshape(count, lanes)


def rows_kernel(
    reach, second, p_ref, r_ref, bh_ref, bl_ref, ch_ref, cl_ref, s_ref, z_ref, taps_ref, mix_ref, modes_ref, out_ref, l_ref, by, mixed
):
    width_x, channels, width_y = s_ref.shape
    odd = lax.axis_index("gx") % 2
    left = 1 - odd if second else odd
    for m in range(reach):
        by[m] = added(reach, left, r_ref, taps_ref, m, channels, width_y)
    rows = halves(by[...].reshape(reach * channels, width_y))
    here = dot2(rows, (bh_ref[...], bl_ref[...])).reshape(by.shape)
    mix = mix_ref[...]
    for m in range(reach):
        mixed[m] = dot(mix, stacked(s_ref[place(reach, left, width_x, m)] + here[m])).astype(BF16)
    over = dot2(rows, (ch_ref[...], cl_ref[...])).reshape(reach, channels, LANES)
    over = [z_ref[place(reach, left, width_x, m)] + over[m] for m in range(reach)]
    over += [jnp.zeros(over[0].shape, F32)] * (-reach % (LANES // (2 * PITCH)))
    packed(l_ref, over)
    total = None
    for m in range(reach):
        term = dot(mixed[m], modes_ref[place(reach, left, width_x, m)])
        total = term if total is None else total + term
    out_ref[...] = p_ref[...] + total


def gather_kernel(reach, core_ref, chip_ref, out_ref, both):
    _, width_x, modes = core_ref.shape
    odd = lax.axis_index("gx") % 2
    gap = jnp.zeros((PITCH - reach, width_x, modes), F32)
    both[:, :PITCH] = jnp.swapaxes(jnp.concatenate([core_ref[...], gap], axis=0), 0, 1)
    both[:, PITCH:] = jnp.swapaxes(jnp.concatenate([chip_ref[...], gap], axis=0), 0, 1)
    inner = width_x - 2 * reach
    room = -(-reach // (LANES // (2 * PITCH))) * (LANES // (2 * PITCH))
    for x in range(inner):
        out_ref[x] = both[reach + x].astype(BF16)
    for i in range(2):
        left = odd if i == 0 else 1 - odd
        for m in range(room):
            if m < reach:
                out_ref[inner + i * room + m] = both[place(reach, left, width_x, m)].astype(BF16)
            else:
                out_ref[inner + i * room + m] = jnp.zeros(out_ref.shape[1:], BF16)


def over_kernel(reach, l0_ref, l1_ref, core_ref, chip_ref, out_ref, blocks_ref, both, blocks):
    gather_kernel(reach, core_ref, chip_ref, blocks, both)
    start = 0
    total = None
    for l_ref in (l0_ref, l1_ref):
        count = l_ref.shape[1] // (2 * PITCH)
        value = over(l_ref[...], blocks[start : start + count])
        total = value if total is None else total + value
        start += count
    out_ref[...] = total
    blocks_ref[...] = blocks[start:]


def over(rows, blocks):
    high = rows.astype(BF16).astype(F32)
    value = dot(jnp.concatenate([high, rows - high], axis=0).astype(BF16), blocks.reshape(-1, blocks.shape[2]))
    half = rows.shape[0]
    return value[:half] + value[half:]


def last_kernel(reach, p_ref, r_ref, o_ref, blocks_ref, *rest):
    *refs, out_ref, total, l_ref, by, mixed = rest
    rows_kernel(reach, True, p_ref, r_ref, *refs, total, l_ref, by, mixed)
    ends = o_ref[...] + over(l_ref[...], blocks_ref[...])
    deliver(total[...] + dot(refs[7][...], stacked(ends)), r_ref.shape[1], out_ref)


def deliver(total, channels, out_ref):
    if len(out_ref.shape) == 2:
        out_ref[...] = total
        return
    _, parts, count, high, lanes = out_ref.shape
    owned = total.shape[1] // parts
    rows = count * high
    for g in range(parts):
        piece = jnp.concatenate(
            [total[k * rows : (k + 1) * rows, g * owned : (g + 1) * owned] for k in range(lanes // owned)], axis=1
        )
        for k in range(out_ref.shape[0]):
            for j in range(count):
                out_ref[k, g, j] = piece[j * high : (j + 1) * high]


def sum_kernel(parts_ref, coefficients_ref, out_ref):
    channels, owned = out_ref.shape
    _, count, high, lanes = parts_ref.shape
    total = jnp.sum(parts_ref[...], axis=0)
    for k in range(lanes // owned):
        for j in range(count):
            rows = pl.ds((k * count + j) * high, high)
            out_ref[rows] = coefficients_ref[rows] + total[j, :, k * owned : (k + 1) * owned]


def vmem(array):
    return pltpu.with_memory_space_constraint(array, pltpu.VMEM)


def call(body, ins, outs, scratch=(), keep=True, outside=False, weight=1e9):
    place_in = pltpu.HBM if outside else pltpu.VMEM
    make = pltpu.VMEM if keep else jax.ShapeDtypeStruct
    return pl.pallas_call(
        body,
        out_shape=[make(shape, dtype) for shape, dtype in outs],
        in_specs=[pl.BlockSpec(memory_space=place_in)] * len(ins),
        out_specs=[pl.BlockSpec(memory_space=pltpu.VMEM)] * len(outs),
        scratch_shapes=list(scratch),
        compiler_params=pltpu.CompilerParams(vmem_limit_bytes=24 << 20),
        cost_estimate=pl.CostEstimate(flops=int(weight), bytes_accessed=1 << 20, transcendentals=0),
    )(*[pltpu.with_memory_space_constraint(array, place_in) for array in ins])


def pairs(count, first):
    found = []
    for low in range(first, count - 1, 2):
        found += [(low, low + 1), (low + 1, low)]
    return found


def local(adjoint_forcing, field_mixing, time_mixing, kernel_east, kernel_north, spatial_modes, coefficients):
    fields, levels, width_x, width_y = adjoint_forcing.shape
    channels, modes, owned = fields * levels, spatial_modes.shape[2], coefficients.shape[0]
    reach = (kernel_east.shape[0] - 1) // 2
    count_x, count_y = lax.axis_size("gx"), lax.axis_size("gy")
    raw = adjoint_forcing.reshape(channels, width_x, width_y)
    slab = ((reach, channels, width_y), F32)
    full = ((width_x, channels, width_y), F32)
    narrow = ((width_x, channels, LANES), F32)
    band = ((width_y, width_y), BF16)
    cross = ((width_y, LANES), BF16)
    wide_rows = -(-channels // 16) * 16
    share = ((wide_rows, modes), F32)
    each = LANES // (2 * PITCH)
    inner = width_x - 2 * reach
    small = [kernel_north.reshape(1, -1), kernel_east.reshape(1, -1), field_mixing, time_mixing]
    s1, *small = call(
        functools.partial(first_kernel, reach),
        [raw, *small],
        [slab] + [(array.shape, F32) for array in small],
        [pltpu.SemaphoreType.DMA((reach + len(small),))],
        outside=True,
        weight=3e9,
    )
    t, s2 = call(functools.partial(turn_kernel, reach), [raw, s1], [full, slab], weight=1e7)
    held = vmem(spatial_modes)
    r1 = lax.ppermute(s1, "gx", pairs(count_x, 0))
    r2 = lax.ppermute(s2, "gx", pairs(count_x, 1))
    y, z, bh, bl, ch, cl = call(
        functools.partial(band_kernel, reach),
        [small[0], t],
        [full, narrow, band, band, cross, cross],
        weight=1e7,
    )
    block = ((reach, width_x, modes), F32)
    core, chip = call(functools.partial(block_kernel, reach), [held], [block, block], weight=3e8)
    core = lax.ppermute(core, "gy", pairs(count_y, 0))
    chip = lax.ppermute(chip, "gy", pairs(count_y, 1))
    s, sz, mix, taps = call(
        functools.partial(own_kernel, reach),
        [*small[1:], y, z],
        [
            full,
            narrow,
            ((wide_rows, 3 * channels + -3 * channels % 96), BF16),
            ((2 * reach + 1, 8, width_y), F32),
        ],
        weight=1e7,
    )
    p, l0 = call(
        functools.partial(tile_kernel, reach),
        [s, sz, mix, held],
        [share, ((channels, inner // each * LANES), F32)],
        weight=1e7,
    )
    both = [bh, bl, ch, cl, s, sz, taps, mix, held]
    layer = (channels, -(-reach // each) * LANES)
    room = [pltpu.VMEM(slab[0], F32), pltpu.VMEM((reach, wide_rows, width_y), BF16)]
    p, l1 = call(
        functools.partial(rows_kernel, reach, False), [p, r1, *both], [share, (layer, F32)], room, weight=1e9
    )
    slots = inner + 2 * (layer[1] // (2 * PITCH))
    ends, blocks = call(
        functools.partial(over_kernel, reach),
        [l0, l1, core, chip],
        [((channels, modes), F32), ((layer[1] // (2 * PITCH), 2 * PITCH, modes), BF16)],
        [pltpu.VMEM((width_x, 2 * PITCH, modes), F32), pltpu.VMEM((slots, 2 * PITCH, modes), BF16)],
        weight=1e7,
    )
    rows = channels * owned // 128
    high = 4 if rows % 4 == 0 else rows
    (out,) = call(
        functools.partial(last_kernel, reach),
        [p, r2, ends, blocks, *both],
        [((count_x, count_y, rows // high, high, 128), F32)],
        [pltpu.VMEM(share[0], F32), pltpu.VMEM(layer, F32), *room],
    )
    out = out.reshape((count_x * count_y,) + out.shape[2:])
    parts = lax.all_to_all(out, ("gx", "gy"), 0, 0, tiled=True)
    (gradient,) = call(sum_kernel, [parts, coefficients.T], [((channels, owned), F32)], keep=False)
    return gradient.T


def solution(mesh):
    in_specs = (P(None, None, "gx", "gy"), P(), P(), P(), P(), P("gx", "gy", None), P("gy", None))
    out_specs = P("gy", None)
    return jax.shard_map(local, mesh=mesh, in_specs=in_specs, out_specs=out_specs, check_vma=False)
```

```python
import functools

import jax
import jax.numpy as jnp
from jax import lax
from jax.experimental import pallas as pl
from jax.experimental.pallas import tpu as pltpu
from jax.sharding import PartitionSpec as P

F32, BF16 = jnp.float32, jnp.bfloat16
NN = (((1,), (0,)), ((), ()))
LANES = 128
PITCH = 16


def dot(a, b, dims=NN):
    return lax.dot_general(a, b, dims, preferred_element_type=F32)


def halves(v):
    high = v.astype(BF16)
    return high, (v - high.astype(F32)).astype(BF16)


def dot2(a, b, dims=NN):
    (ah, al), (bh, bl) = a, b
    return dot(ah, bh, dims) + dot(ah, bl, dims) + dot(al, bh, dims)


def iota(shape, dim):
    return lax.broadcasted_iota(jnp.int32, shape, dim)


def stacked(v):
    high = v.astype(BF16).astype(F32)
    parts = [high, v - high, high]
    if (3 * v.shape[0]) % 16:
        parts.append(jnp.zeros((-3 * v.shape[0] % 96, v.shape[1]), F32))
    return jnp.concatenate(parts, axis=0).astype(BF16)


def wide(m):
    high = m.astype(BF16).astype(F32)
    parts = [high, high, m - high]
    if (3 * m.shape[1]) % 16:
        parts.append(jnp.zeros((m.shape[0], -3 * m.shape[1] % 96), F32))
    return jnp.concatenate(parts, axis=1).astype(BF16)


def first_kernel(reach, a_hbm, *refs):
    count = (len(refs) - 2) // 2
    small, s1_ref, held, sem = refs[:count], refs[count], refs[count + 1 : -1], refs[-1]
    odd = lax.axis_index("gx") % 2
    far = a_hbm.shape[1] - reach
    copies = [pltpu.make_async_copy(x, y, sem.at[i]) for i, (x, y) in enumerate(zip(small, held))]

    def rows(start):
        return [pltpu.make_async_copy(a_hbm.at[:, start + n], s1_ref.at[n], sem.at[count + n]) for n in range(reach)]

    for left in range(2):

        @pl.when(odd == left)
        def _():
            for copy in rows((1 - left) * far):
                copy.start()

    for copy in copies:
        copy.start()
    for left in range(2):

        @pl.when(odd == left)
        def _():
            for copy in rows((1 - left) * far):
                copy.wait()

    for copy in copies:
        copy.wait()


def second_kernel(reach, a_ref, before_ref, s2_ref):
    del before_ref
    width_x = a_ref.shape[1]
    window = -(-reach // 8) * 8
    odd = lax.axis_index("gx") % 2
    rows = a_ref[:, pl.ds(pl.multiple_of(odd * (width_x - window), 8), window)]
    rows = jnp.swapaxes(rows, 0, 1)
    s2_ref[...] = jnp.where(odd == 1, rows[window - reach :], rows[:reach])


def turn_kernel(a_ref, before_ref, t_ref):
    del before_ref
    t_ref[...] = jnp.swapaxes(a_ref[...], 0, 1)


def block_kernel(reach, modes_ref, core_ref, chip_ref):
    width_y = modes_ref.shape[1]
    odd = lax.axis_index("gy") % 2
    low = jnp.swapaxes(modes_ref[:, :PITCH].astype(F32), 0, 1)
    high = jnp.swapaxes(modes_ref[:, width_y - PITCH :].astype(F32), 0, 1)
    for i in range(reach):
        a, b = low[i], high[PITCH - reach + i]
        core_ref[i] = jnp.where(odd == 1, a, b)
        chip_ref[i] = jnp.where(odd == 1, b, a)


def band_kernel(reach, north_ref, t_ref, y_ref, z_ref, bh_ref, bl_ref, ch_ref, cl_ref):
    width_x, channels, width_y = t_ref.shape
    span = 2 * reach + 1
    odd = lax.axis_index("gy") % 2
    shift = iota((width_y, width_y), 0) - iota((width_y, width_y), 1) + reach
    lane = iota((width_y, LANES), 1)
    at = lane % PITCH
    right = jnp.where(lane < PITCH, 1 - odd, odd) == 1
    over = iota((width_y, LANES), 0) - at + jnp.where(right, reach - width_y, 2 * reach)
    over = jnp.where((at < reach) & (lane < 2 * PITCH), over, -1)
    first = iota((8, width_y), 1)
    base = jnp.zeros((8, width_y), F32)
    cross = jnp.zeros((width_y, LANES), F32)
    for j in range(span):
        tap = north_ref[:, j : j + 1]
        base = jnp.where(first == (reach - j) % width_y, tap, base)
        cross = jnp.where(over == j, tap, cross)
    rolled = pltpu.roll(jnp.broadcast_to(base[:1], (width_y, width_y)), 0, 1, stride=1, stride_axis=0)
    band = halves(jnp.where((shift >= 0) & (shift < span), rolled, 0.0))
    cross = halves(cross)
    bh_ref[...], bl_ref[...] = band
    ch_ref[...], cl_ref[...] = cross
    data = halves(t_ref[...].reshape(width_x * channels, width_y))
    y_ref[...] = dot2(data, band).reshape(y_ref.shape)
    z_ref[...] = dot2(data, cross).reshape(z_ref.shape)


def own_kernel(reach, east_ref, field_ref, time_ref, y_ref, z_ref, s_ref, sz_ref, mix_ref, taps_ref):
    width_x, channels, width_y = y_ref.shape
    x_shift = iota((width_x, width_x), 1) - iota((width_x, width_x), 0) + reach
    along = jnp.zeros((width_x, width_x), F32)
    for j in range(2 * reach + 1):
        tap = east_ref[:, j : j + 1]
        along = jnp.where(x_shift == j, tap, along)
        taps_ref[j] = jnp.broadcast_to(tap, taps_ref.shape[1:])
    along = wide(along)
    s_ref[...] = along_x(along, y_ref[...])
    sz_ref[...] = along_x(along, z_ref[...])
    fields, levels = field_ref.shape[0], time_ref.shape[0]
    rows = mix_ref.shape[0]
    out, into = iota((rows, channels), 0), iota((rows, channels), 1)
    by_field = jnp.zeros((rows, channels), F32)
    by_time = jnp.zeros((rows, channels), F32)
    for g in range(fields):
        for f in range(fields):
            here = (into // levels == g) & (out // levels == f)
            by_field = jnp.where(here, field_ref[g : g + 1, f : f + 1], by_field)
    for s in range(levels):
        for t in range(levels):
            here = (into % levels == s) & (out % levels == t)
            by_time = jnp.where(here, time_ref[s : s + 1, t : t + 1], by_time)
    mix_ref[...] = wide(by_field * by_time)


def along_x(matrix, y):
    by_channel = jnp.swapaxes(y, 0, 1)
    return jnp.swapaxes(jnp.stack([dot(matrix, stacked(by_channel[c])) for c in range(y.shape[1])]), 0, 1)


def tile_kernel(reach, s_ref, z_ref, mix_ref, modes_ref, p_ref, l_ref):
    width_x = s_ref.shape[0]
    mix = mix_ref[...]
    inner = [dot(mix, stacked(s_ref[x])).astype(BF16) for x in range(reach, width_x - reach)]
    acc = dot(inner[0], modes_ref[reach])
    for x in range(1, width_x - 2 * reach):
        acc = acc + dot(inner[x], modes_ref[reach + x])
    p_ref[...] = acc
    packed(l_ref, [z_ref[x] for x in range(reach, width_x - reach)])


def packed(l_ref, values):
    each = LANES // (2 * PITCH)
    for tile in range(l_ref.shape[1] // LANES):
        total = None
        for k, value in enumerate(values[tile * each : (tile + 1) * each]):
            value = pltpu.roll(value, k * 2 * PITCH, 1) if k else value
            total = value if total is None else total + value
        l_ref[:, tile * LANES : (tile + 1) * LANES] = total


def place(reach, left, width_x, m):
    return left * (reach - 1 - m) + (1 - left) * (width_x - reach + m)


def added(reach, left, rows, taps_ref, m, count, lanes):
    value = None
    for n in range(m + 1):
        d = m - n
        tap = taps_ref[left * d + (1 - left) * (2 * reach - d), :, :lanes][None]
        term = tap * rows[left * (reach - 1 - n) + (1 - left) * n].reshape(count // 8, 8, lanes)
        value = term if value is None else value + term
    return value.reshape(count, lanes)


def rows_kernel(
    reach, second, p_ref, r_ref, bh_ref, bl_ref, ch_ref, cl_ref, s_ref, z_ref, taps_ref, mix_ref, modes_ref, out_ref, l_ref, by, mixed
):
    width_x, channels, width_y = s_ref.shape
    odd = lax.axis_index("gx") % 2
    left = 1 - odd if second else odd
    for m in range(reach):
        by[m] = added(reach, left, r_ref, taps_ref, m, channels, width_y)
    rows = halves(by[...].reshape(reach * channels, width_y))
    here = dot2(rows, (bh_ref[...], bl_ref[...])).reshape(by.shape)
    mix = mix_ref[...]
    for m in range(reach):
        mixed[m] = dot(mix, stacked(s_ref[place(reach, left, width_x, m)] + here[m])).astype(BF16)
    over = dot2(rows, (ch_ref[...], cl_ref[...])).reshape(reach, channels, LANES)
    over = [z_ref[place(reach, left, width_x, m)] + over[m] for m in range(reach)]
    over += [jnp.zeros(over[0].shape, F32)] * (-reach % (LANES // (2 * PITCH)))
    packed(l_ref, over)
    total = None
    for m in range(reach):
        term = dot(mixed[m], modes_ref[place(reach, left, width_x, m)])
        total = term if total is None else total + term
    out_ref[...] = p_ref[...] + total


def gather_kernel(reach, core_ref, chip_ref, out_ref, both):
    _, width_x, modes = core_ref.shape
    odd = lax.axis_index("gx") % 2
    gap = jnp.zeros((PITCH - reach, width_x, modes), F32)
    both[:, :PITCH] = jnp.swapaxes(jnp.concatenate([core_ref[...], gap], axis=0), 0, 1)
    both[:, PITCH:] = jnp.swapaxes(jnp.concatenate([chip_ref[...], gap], axis=0), 0, 1)
    inner = width_x - 2 * reach
    room = -(-reach // (LANES // (2 * PITCH))) * (LANES // (2 * PITCH))
    for x in range(inner):
        out_ref[x] = both[reach + x].astype(BF16)
    for i in range(2):
        left = odd if i == 0 else 1 - odd
        for m in range(room):
            if m < reach:
                out_ref[inner + i * room + m] = both[place(reach, left, width_x, m)].astype(BF16)
            else:
                out_ref[inner + i * room + m] = jnp.zeros(out_ref.shape[1:], BF16)


def over_kernel(reach, l0_ref, l1_ref, core_ref, chip_ref, out_ref, blocks_ref, both, blocks):
    gather_kernel(reach, core_ref, chip_ref, blocks, both)
    start = 0
    total = None
    for l_ref in (l0_ref, l1_ref):
        count = l_ref.shape[1] // (2 * PITCH)
        value = over(l_ref[...], blocks[start : start + count])
        total = value if total is None else total + value
        start += count
    out_ref[...] = total
    blocks_ref[...] = blocks[start:]


def over(rows, blocks):
    high = rows.astype(BF16).astype(F32)
    value = dot(jnp.concatenate([high, rows - high], axis=0).astype(BF16), blocks.reshape(-1, blocks.shape[2]))
    half = rows.shape[0]
    return value[:half] + value[half:]


def last_kernel(reach, p_ref, r_ref, o_ref, blocks_ref, *rest):
    *refs, out_ref, total, l_ref, by, mixed = rest
    rows_kernel(reach, True, p_ref, r_ref, *refs, total, l_ref, by, mixed)
    ends = o_ref[...] + over(l_ref[...], blocks_ref[...])
    deliver(total[...] + dot(refs[7][...], stacked(ends)), r_ref.shape[1], out_ref)


def deliver(total, channels, out_ref):
    if len(out_ref.shape) == 2:
        out_ref[...] = total
        return
    _, parts, count, high, lanes = out_ref.shape
    owned = total.shape[1] // parts
    rows = count * high
    for g in range(parts):
        piece = jnp.concatenate(
            [total[k * rows : (k + 1) * rows, g * owned : (g + 1) * owned] for k in range(lanes // owned)], axis=1
        )
        for k in range(out_ref.shape[0]):
            for j in range(count):
                out_ref[k, g, j] = piece[j * high : (j + 1) * high]


def sum_kernel(parts_ref, coefficients_ref, out_ref):
    channels, owned = out_ref.shape
    _, count, high, lanes = parts_ref.shape
    total = jnp.sum(parts_ref[...], axis=0)
    for k in range(lanes // owned):
        for j in range(count):
            rows = pl.ds((k * count + j) * high, high)
            out_ref[rows] = coefficients_ref[rows] + total[j, :, k * owned : (k + 1) * owned]


def vmem(array):
    return pltpu.with_memory_space_constraint(array, pltpu.VMEM)


def call(body, ins, outs, scratch=(), keep=True, outside=False, weight=1e9):
    place_in = pltpu.HBM if outside else pltpu.VMEM
    make = pltpu.VMEM if keep else jax.ShapeDtypeStruct
    return pl.pallas_call(
        body,
        out_shape=[make(shape, dtype) for shape, dtype in outs],
        in_specs=[pl.BlockSpec(memory_space=place_in)] * len(ins),
        out_specs=[pl.BlockSpec(memory_space=pltpu.VMEM)] * len(outs),
        scratch_shapes=list(scratch),
        compiler_params=pltpu.CompilerParams(vmem_limit_bytes=24 << 20),
        cost_estimate=pl.CostEstimate(flops=int(weight), bytes_accessed=1 << 20, transcendentals=0),
    )(*[pltpu.with_memory_space_constraint(array, place_in) for array in ins])


def pairs(count, first):
    found = []
    for low in range(first, count - 1, 2):
        found += [(low, low + 1), (low + 1, low)]
    return found


def local(adjoint_forcing, field_mixing, time_mixing, kernel_east, kernel_north, spatial_modes, coefficients):
    fields, levels, width_x, width_y = adjoint_forcing.shape
    channels, modes, owned = fields * levels, spatial_modes.shape[2], coefficients.shape[0]
    reach = (kernel_east.shape[0] - 1) // 2
    count_x, count_y = lax.axis_size("gx"), lax.axis_size("gy")
    raw = adjoint_forcing.reshape(channels, width_x, width_y)
    slab = ((reach, channels, width_y), F32)
    full = ((width_x, channels, width_y), F32)
    narrow = ((width_x, channels, LANES), F32)
    band = ((width_y, width_y), BF16)
    cross = ((width_y, LANES), BF16)
    wide_rows = -(-channels // 16) * 16
    share = ((wide_rows, modes), F32)
    each = LANES // (2 * PITCH)
    inner = width_x - 2 * reach
    small = [kernel_north.reshape(1, -1), kernel_east.reshape(1, -1), field_mixing, time_mixing]
    s1, *small = call(
        functools.partial(first_kernel, reach),
        [raw, *small],
        [slab] + [(array.shape, F32) for array in small],
        [pltpu.SemaphoreType.DMA((reach + len(small),))],
        outside=True,
        weight=3e9,
    )
    raw = vmem(raw)
    (s2,) = call(functools.partial(second_kernel, reach), [raw, s1], [slab], weight=1e7)
    (t,) = call(turn_kernel, [raw, s2], [full], weight=1e7)
    held = vmem(spatial_modes)
    r1 = lax.ppermute(s1, "gx", pairs(count_x, 0))
    r2 = lax.ppermute(s2, "gx", pairs(count_x, 1))
    y, z, bh, bl, ch, cl = call(
        functools.partial(band_kernel, reach),
        [small[0], t],
        [full, narrow, band, band, cross, cross],
        weight=1e7,
    )
    block = ((reach, width_x, modes), F32)
    core, chip = call(functools.partial(block_kernel, reach), [held], [block, block], weight=3e8)
    core = lax.ppermute(core, "gy", pairs(count_y, 0))
    chip = lax.ppermute(chip, "gy", pairs(count_y, 1))
    s, sz, mix, taps = call(
        functools.partial(own_kernel, reach),
        [*small[1:], y, z],
        [
            full,
            narrow,
            ((wide_rows, 3 * channels + -3 * channels % 96), BF16),
            ((2 * reach + 1, 8, width_y), F32),
        ],
        weight=1e7,
    )
    p, l0 = call(
        functools.partial(tile_kernel, reach),
        [s, sz, mix, held],
        [share, ((channels, inner // each * LANES), F32)],
        weight=1e7,
    )
    both = [bh, bl, ch, cl, s, sz, taps, mix, held]
    layer = (channels, -(-reach // each) * LANES)
    room = [pltpu.VMEM(slab[0], F32), pltpu.VMEM((reach, wide_rows, width_y), BF16)]
    p, l1 = call(
        functools.partial(rows_kernel, reach, False), [p, r1, *both], [share, (layer, F32)], room, weight=1e9
    )
    slots = inner + 2 * (layer[1] // (2 * PITCH))
    ends, blocks = call(
        functools.partial(over_kernel, reach),
        [l0, l1, core, chip],
        [((channels, modes), F32), ((layer[1] // (2 * PITCH), 2 * PITCH, modes), BF16)],
        [pltpu.VMEM((width_x, 2 * PITCH, modes), F32), pltpu.VMEM((slots, 2 * PITCH, modes), BF16)],
        weight=1e7,
    )
    rows = channels * owned // 128
    high = 4 if rows % 4 == 0 else rows
    (out,) = call(
        functools.partial(last_kernel, reach),
        [p, r2, ends, blocks, *both],
        [((count_x, count_y, rows // high, high, 128), F32)],
        [pltpu.VMEM(share[0], F32), pltpu.VMEM(layer, F32), *room],
    )
    out = out.reshape((count_x * count_y,) + out.shape[2:])
    parts = lax.all_to_all(out, ("gx", "gy"), 0, 0, tiled=True)
    (gradient,) = call(sum_kernel, [parts, coefficients.T], [((channels, owned), F32)], keep=False)
    return gradient.T


def solution(mesh):
    in_specs = (P(None, None, "gx", "gy"), P(), P(), P(), P(), P("gx", "gy", None), P("gy", None))
    out_specs = P("gy", None)
    return jax.shard_map(local, mesh=mesh, in_specs=in_specs, out_specs=out_specs, check_vma=False)
```

```python
import functools

import jax
import jax.numpy as jnp
from jax import lax
from jax.experimental import pallas as pl
from jax.experimental.pallas import tpu as pltpu
from jax.sharding import PartitionSpec as P

F32, BF16 = jnp.float32, jnp.bfloat16
NN = (((1,), (0,)), ((), ()))
LANES = 128
PITCH = 16


def dot(a, b, dims=NN):
    return lax.dot_general(a, b, dims, preferred_element_type=F32)


def halves(v):
    high = v.astype(BF16)
    return high, (v - high.astype(F32)).astype(BF16)


def dot2(a, b, dims=NN):
    (ah, al), (bh, bl) = a, b
    return dot(ah, bh, dims) + dot(ah, bl, dims) + dot(al, bh, dims)


def iota(shape, dim):
    return lax.broadcasted_iota(jnp.int32, shape, dim)


def stacked(v):
    high = v.astype(BF16).astype(F32)
    parts = [high, v - high, high]
    if (3 * v.shape[0]) % 16:
        parts.append(jnp.zeros((-3 * v.shape[0] % 16, v.shape[1]), F32))
    return jnp.concatenate(parts, axis=0).astype(BF16)


def wide(m):
    high = m.astype(BF16).astype(F32)
    parts = [high, high, m - high]
    if (3 * m.shape[1]) % 16:
        parts.append(jnp.zeros((m.shape[0], -3 * m.shape[1] % 16), F32))
    return jnp.concatenate(parts, axis=1).astype(BF16)


def first_kernel(reach, a_hbm, *refs):
    count = (len(refs) - 2) // 2
    small, s1_ref, held, sem = refs[:count], refs[count], refs[count + 1 : -1], refs[-1]
    odd = lax.axis_index("gx") % 2
    far = a_hbm.shape[1] - reach
    copies = [pltpu.make_async_copy(x, y, sem.at[i]) for i, (x, y) in enumerate(zip(small, held))]

    def rows(start):
        return [pltpu.make_async_copy(a_hbm.at[:, start + n], s1_ref.at[n], sem.at[count + n]) for n in range(reach)]

    for left in range(2):

        @pl.when(odd == left)
        def _():
            for copy in rows((1 - left) * far):
                copy.start()

    for copy in copies:
        copy.start()
    for left in range(2):

        @pl.when(odd == left)
        def _():
            for copy in rows((1 - left) * far):
                copy.wait()

    for copy in copies:
        copy.wait()


def turn_kernel(reach, a_ref, before_ref, t_ref, s2_ref):
    del before_ref
    t_ref[...] = jnp.swapaxes(a_ref[...], 0, 1)
    s2_ref[...] = t_ref[pl.ds(lax.axis_index("gx") % 2 * (t_ref.shape[0] - reach), reach)]


def block_kernel(reach, modes_ref, core_ref, chip_ref):
    width_y = modes_ref.shape[1]
    odd = lax.axis_index("gy") % 2
    low = jnp.swapaxes(modes_ref[:, :PITCH].astype(F32), 0, 1)
    high = jnp.swapaxes(modes_ref[:, width_y - PITCH :].astype(F32), 0, 1)
    for i in range(reach):
        a, b = low[i], high[PITCH - reach + i]
        core_ref[i] = jnp.where(odd == 1, a, b)
        chip_ref[i] = jnp.where(odd == 1, b, a)


def band_kernel(reach, north_ref, t_ref, y_ref, z_ref, bh_ref, bl_ref, ch_ref, cl_ref):
    width_x, channels, width_y = t_ref.shape
    span = 2 * reach + 1
    odd = lax.axis_index("gy") % 2
    shift = iota((width_y, width_y), 0) - iota((width_y, width_y), 1) + reach
    lane = iota((width_y, LANES), 1)
    at = lane % PITCH
    right = jnp.where(lane < PITCH, 1 - odd, odd) == 1
    over = iota((width_y, LANES), 0) - at + jnp.where(right, reach - width_y, 2 * reach)
    over = jnp.where((at < reach) & (lane < 2 * PITCH), over, -1)
    first = iota((8, width_y), 1)
    base = jnp.zeros((8, width_y), F32)
    cross = jnp.zeros((width_y, LANES), F32)
    for j in range(span):
        tap = north_ref[:, j : j + 1]
        base = jnp.where(first == (reach - j) % width_y, tap, base)
        cross = jnp.where(over == j, tap, cross)
    rolled = pltpu.roll(jnp.broadcast_to(base[:1], (width_y, width_y)), 0, 1, stride=1, stride_axis=0)
    band = halves(jnp.where((shift >= 0) & (shift < span), rolled, 0.0))
    cross = halves(cross)
    bh_ref[...], bl_ref[...] = band
    ch_ref[...], cl_ref[...] = cross
    data = halves(t_ref[...].reshape(width_x * channels, width_y))
    y_ref[...] = dot2(data, band).reshape(y_ref.shape)
    z_ref[...] = dot2(data, cross).reshape(z_ref.shape)


def own_kernel(reach, east_ref, field_ref, time_ref, y_ref, z_ref, s_ref, sz_ref, mix_ref, taps_ref):
    width_x, channels, width_y = y_ref.shape
    x_shift = iota((width_x, width_x), 1) - iota((width_x, width_x), 0) + reach
    along = jnp.zeros((width_x, width_x), F32)
    for j in range(2 * reach + 1):
        tap = east_ref[:, j : j + 1]
        along = jnp.where(x_shift == j, tap, along)
        taps_ref[j] = jnp.broadcast_to(tap, taps_ref.shape[1:])
    along = wide(along)
    s_ref[...] = along_x(along, y_ref[...])
    sz_ref[...] = along_x(along, z_ref[...])
    fields, levels = field_ref.shape[0], time_ref.shape[0]
    rows = mix_ref.shape[0]
    out, into = iota((rows, channels), 0), iota((rows, channels), 1)
    by_field = jnp.zeros((rows, channels), F32)
    by_time = jnp.zeros((rows, channels), F32)
    for g in range(fields):
        for f in range(fields):
            here = (into // levels == g) & (out // levels == f)
            by_field = jnp.where(here, field_ref[g : g + 1, f : f + 1], by_field)
    for s in range(levels):
        for t in range(levels):
            here = (into % levels == s) & (out % levels == t)
            by_time = jnp.where(here, time_ref[s : s + 1, t : t + 1], by_time)
    mix_ref[...] = wide(by_field * by_time)


def along_x(matrix, y):
    by_channel = jnp.swapaxes(y, 0, 1)
    return jnp.swapaxes(jnp.stack([dot(matrix, stacked(by_channel[c])) for c in range(y.shape[1])]), 0, 1)


def tile_kernel(reach, s_ref, z_ref, mix_ref, modes_ref, p_ref, l_ref):
    width_x = s_ref.shape[0]
    mix = mix_ref[...]
    inner = [dot(mix, stacked(s_ref[x])).astype(BF16) for x in range(reach, width_x - reach)]
    acc = dot(inner[0], modes_ref[reach])
    for x in range(1, width_x - 2 * reach):
        acc = acc + dot(inner[x], modes_ref[reach + x])
    p_ref[...] = acc
    packed(l_ref, [z_ref[x] for x in range(reach, width_x - reach)])


def packed(l_ref, values):
    each = LANES // (2 * PITCH)
    for tile in range(l_ref.shape[1] // LANES):
        total = None
        for k, value in enumerate(values[tile * each : (tile + 1) * each]):
            value = pltpu.roll(value, k * 2 * PITCH, 1) if k else value
            total = value if total is None else total + value
        l_ref[:, tile * LANES : (tile + 1) * LANES] = total


def place(reach, left, width_x, m):
    return left * (reach - 1 - m) + (1 - left) * (width_x - reach + m)


def added(reach, left, rows, taps_ref, m, count, lanes):
    value = None
    for n in range(m + 1):
        d = m - n
        tap = taps_ref[left * d + (1 - left) * (2 * reach - d), :, :lanes][None]
        term = tap * rows[left * (reach - 1 - n) + (1 - left) * n].reshape(count // 8, 8, lanes)
        value = term if value is None else value + term
    return value.reshape(count, lanes)


def rows_kernel(
    reach, second, p_ref, r_ref, bh_ref, bl_ref, ch_ref, cl_ref, s_ref, z_ref, taps_ref, mix_ref, modes_ref, out_ref, l_ref, by, mixed
):
    width_x, channels, width_y = s_ref.shape
    odd = lax.axis_index("gx") % 2
    left = 1 - odd if second else odd
    for m in range(reach):
        by[m] = added(reach, left, r_ref, taps_ref, m, channels, width_y)
    rows = halves(by[...].reshape(reach * channels, width_y))
    here = dot2(rows, (bh_ref[...], bl_ref[...])).reshape(by.shape)
    mix = mix_ref[...]
    for m in range(reach):
        mixed[m] = dot(mix, stacked(s_ref[place(reach, left, width_x, m)] + here[m])).astype(BF16)
    over = dot2(rows, (ch_ref[...], cl_ref[...])).reshape(reach, channels, LANES)
    over = [z_ref[place(reach, left, width_x, m)] + over[m] for m in range(reach)]
    over += [jnp.zeros(over[0].shape, F32)] * (-reach % (LANES // (2 * PITCH)))
    packed(l_ref, over)
    total = None
    for m in range(reach):
        term = dot(mixed[m], modes_ref[place(reach, left, width_x, m)])
        total = term if total is None else total + term
    out_ref[...] = p_ref[...] + total


def gather_kernel(reach, core_ref, chip_ref, out_ref, both):
    _, width_x, modes = core_ref.shape
    odd = lax.axis_index("gx") % 2
    gap = jnp.zeros((PITCH - reach, width_x, modes), F32)
    both[:, :PITCH] = jnp.swapaxes(jnp.concatenate([core_ref[...], gap], axis=0), 0, 1)
    both[:, PITCH:] = jnp.swapaxes(jnp.concatenate([chip_ref[...], gap], axis=0), 0, 1)
    inner = width_x - 2 * reach
    room = -(-reach // (LANES // (2 * PITCH))) * (LANES // (2 * PITCH))
    for x in range(inner):
        out_ref[x] = both[reach + x].astype(BF16)
    for i in range(2):
        left = odd if i == 0 else 1 - odd
        for m in range(room):
            if m < reach:
                out_ref[inner + i * room + m] = both[place(reach, left, width_x, m)].astype(BF16)
            else:
                out_ref[inner + i * room + m] = jnp.zeros(out_ref.shape[1:], BF16)


def over_kernel(reach, l0_ref, l1_ref, core_ref, chip_ref, out_ref, blocks_ref, both, blocks):
    gather_kernel(reach, core_ref, chip_ref, blocks, both)
    start = 0
    total = None
    for l_ref in (l0_ref, l1_ref):
        count = l_ref.shape[1] // (2 * PITCH)
        value = over(l_ref[...], blocks[start : start + count])
        total = value if total is None else total + value
        start += count
    out_ref[...] = total
    blocks_ref[...] = blocks[start:]


def over(rows, blocks):
    high = rows.astype(BF16).astype(F32)
    value = dot(jnp.concatenate([high, rows - high], axis=0).astype(BF16), blocks.reshape(-1, blocks.shape[2]))
    half = rows.shape[0]
    return value[:half] + value[half:]


def last_kernel(reach, p_ref, r_ref, o_ref, blocks_ref, *rest):
    *refs, out_ref, total, l_ref, by, mixed = rest
    rows_kernel(reach, True, p_ref, r_ref, *refs, total, l_ref, by, mixed)
    ends = o_ref[...] + over(l_ref[...], blocks_ref[...])
    deliver(total[...] + dot(refs[7][...], stacked(ends)), r_ref.shape[1], out_ref)


def deliver(total, channels, out_ref):
    if len(out_ref.shape) == 2:
        out_ref[...] = total
        return
    _, parts, count, high, lanes = out_ref.shape
    owned = total.shape[1] // parts
    rows = count * high
    for g in range(parts):
        piece = jnp.concatenate(
            [total[k * rows : (k + 1) * rows, g * owned : (g + 1) * owned] for k in range(lanes // owned)], axis=1
        )
        for k in range(out_ref.shape[0]):
            for j in range(count):
                out_ref[k, g, j] = piece[j * high : (j + 1) * high]


def sum_kernel(parts_ref, coefficients_ref, out_ref):
    channels, owned = out_ref.shape
    _, count, high, lanes = parts_ref.shape
    total = jnp.sum(parts_ref[...], axis=0)
    for k in range(lanes // owned):
        for j in range(count):
            rows = pl.ds((k * count + j) * high, high)
            out_ref[rows] = coefficients_ref[rows] + total[j, :, k * owned : (k + 1) * owned]


def vmem(array):
    return pltpu.with_memory_space_constraint(array, pltpu.VMEM)


def call(body, ins, outs, scratch=(), keep=True, outside=False, weight=1e9):
    place_in = pltpu.HBM if outside else pltpu.VMEM
    make = pltpu.VMEM if keep else jax.ShapeDtypeStruct
    return pl.pallas_call(
        body,
        out_shape=[make(shape, dtype) for shape, dtype in outs],
        in_specs=[pl.BlockSpec(memory_space=place_in)] * len(ins),
        out_specs=[pl.BlockSpec(memory_space=pltpu.VMEM)] * len(outs),
        scratch_shapes=list(scratch),
        compiler_params=pltpu.CompilerParams(vmem_limit_bytes=24 << 20),
        cost_estimate=pl.CostEstimate(flops=int(weight), bytes_accessed=1 << 20, transcendentals=0),
    )(*[pltpu.with_memory_space_constraint(array, place_in) for array in ins])


def pairs(count, first):
    found = []
    for low in range(first, count - 1, 2):
        found += [(low, low + 1), (low + 1, low)]
    return found


def local(adjoint_forcing, field_mixing, time_mixing, kernel_east, kernel_north, spatial_modes, coefficients):
    fields, levels, width_x, width_y = adjoint_forcing.shape
    channels, modes, owned = fields * levels, spatial_modes.shape[2], coefficients.shape[0]
    reach = (kernel_east.shape[0] - 1) // 2
    count_x, count_y = lax.axis_size("gx"), lax.axis_size("gy")
    raw = adjoint_forcing.reshape(channels, width_x, width_y)
    slab = ((reach, channels, width_y), F32)
    full = ((width_x, channels, width_y), F32)
    narrow = ((width_x, channels, LANES), F32)
    band = ((width_y, width_y), BF16)
    cross = ((width_y, LANES), BF16)
    wide_rows = -(-channels // 16) * 16
    share = ((wide_rows, modes), F32)
    each = LANES // (2 * PITCH)
    inner = width_x - 2 * reach
    small = [kernel_north.reshape(1, -1), kernel_east.reshape(1, -1), field_mixing, time_mixing]
    s1, *small = call(
        functools.partial(first_kernel, reach),
        [raw, *small],
        [slab] + [(array.shape, F32) for array in small],
        [pltpu.SemaphoreType.DMA((reach + len(small),))],
        outside=True,
        weight=3e9,
    )
    t, s2 = call(functools.partial(turn_kernel, reach), [raw, s1], [full, slab], weight=1e7)
    held = vmem(spatial_modes)
    r1 = lax.ppermute(s1, "gx", pairs(count_x, 0))
    r2 = lax.ppermute(s2, "gx", pairs(count_x, 1))
    y, z, bh, bl, ch, cl = call(
        functools.partial(band_kernel, reach),
        [small[0], t],
        [full, narrow, band, band, cross, cross],
        weight=1e7,
    )
    block = ((reach, width_x, modes), F32)
    core, chip = call(functools.partial(block_kernel, reach), [held], [block, block], weight=3e8)
    core = lax.ppermute(core, "gy", pairs(count_y, 0))
    chip = lax.ppermute(chip, "gy", pairs(count_y, 1))
    s, sz, mix, taps = call(
        functools.partial(own_kernel, reach),
        [*small[1:], y, z],
        [
            full,
            narrow,
            ((wide_rows, 3 * channels + -3 * channels % 16), BF16),
            ((2 * reach + 1, 8, width_y), F32),
        ],
        weight=1e7,
    )
    p, l0 = call(
        functools.partial(tile_kernel, reach),
        [s, sz, mix, held],
        [share, ((channels, inner // each * LANES), F32)],
        weight=1e7,
    )
    both = [bh, bl, ch, cl, s, sz, taps, mix, held]
    layer = (channels, -(-reach // each) * LANES)
    room = [pltpu.VMEM(slab[0], F32), pltpu.VMEM((reach, wide_rows, width_y), BF16)]
    p, l1 = call(
        functools.partial(rows_kernel, reach, False), [p, r1, *both], [share, (layer, F32)], room, weight=1e9
    )
    slots = inner + 2 * (layer[1] // (2 * PITCH))
    ends, blocks = call(
        functools.partial(over_kernel, reach),
        [l0, l1, core, chip],
        [((channels, modes), F32), ((layer[1] // (2 * PITCH), 2 * PITCH, modes), BF16)],
        [pltpu.VMEM((width_x, 2 * PITCH, modes), F32), pltpu.VMEM((slots, 2 * PITCH, modes), BF16)],
        weight=1e7,
    )
    rows = channels * owned // 128
    high = 4 if rows % 4 == 0 else rows
    (out,) = call(
        functools.partial(last_kernel, reach),
        [p, r2, ends, blocks, *both],
        [((count_x, count_y, rows // high, high, 128), F32)],
        [pltpu.VMEM(share[0], F32), pltpu.VMEM(layer, F32), *room],
    )
    out = out.reshape((count_x * count_y,) + out.shape[2:])
    parts = lax.all_to_all(out, ("gx", "gy"), 0, 0, tiled=True)
    (gradient,) = call(sum_kernel, [parts, coefficients.T], [((channels, owned), F32)], keep=False)
    return gradient.T


def solution(mesh):
    in_specs = (P(None, None, "gx", "gy"), P(), P(), P(), P(), P("gx", "gy", None), P("gy", None))
    out_specs = P("gy", None)
    return jax.shard_map(local, mesh=mesh, in_specs=in_specs, out_specs=out_specs, check_vma=False)
```
